256 devices in a mesh: ctx: 32 (over z, y_hi, core), tp: 8 (over y_lo, x).
Axes of the slice: x: 4, y: 4 (y_hi: 2, y_lo: 2; y = y_hi * 2 + y_lo), z: 8, core: 2. Of those that a mesh axis runs over, the one named last changes fastest.
Arguments:
- queries: bfloat16 [8192, 4096], P('ctx', 'tp'), may hold values from -44 to 44
- keys: bfloat16 [8192, 1024], P('ctx', 'tp'), may hold values from -24 to 24
- values: bfloat16 [8192, 1024], P('ctx', 'tp'), may hold values from -6 to 6
- grad_out: bfloat16 [8192, 4096], P('ctx', 'tp'), may hold values from -6 to 6
- doc_lengths: int32 [17], replicated, may hold values from 1 to 4352, as said below
Outputs:
- grad_queries: bfloat16 [8192, 4096], P(('ctx', 'tp'))
- grad_keys: bfloat16 [8192, 1024], P(('ctx', 'tp'))
- grad_values: bfloat16 [8192, 1024], P(('ctx', 'tp'))
The draws below stay inside these ranges and needn't reach their ends.
Inputs may be any that keep to these rules, and one draw needn't show every extreme that they name: `doc_lengths`: 17 documents fill the 8192 positions; the longest has exactly 4352 tokens.
All inputs are finite; a program needn't handle non-finite values.
Results may differ from the reference program's by a relative error of at most 0.008.
Values may be sent and summed in bfloat16 or wider, within the bound.
No kernel may reach another device: no remote copies, remote signals or barrier semaphores. Data moves between devices by JAX's collectives and lax.ppermute only.
A program may use at most 64 MiB of HBM per device.

```python
import math
import jax
import jax.numpy as jnp
from jax import lax

QH = 32
KH = 8
HD = 128
GROUP = 4
TOK_DEV = 256
DOC_MAX = 4352
TOKENS = 8192
DOCS = 17


def shared_parts(key):
    pieces = jax.random.split(key, 5)
    drawn = jnp.clip(jax.random.normal(pieces[0], (TOKENS, KH * HD), jnp.float32), -6.0, 6.0)
    spread = jnp.exp(jax.random.uniform(pieces[4], (TOKENS, 1), jnp.float32, math.log(0.4), math.log(4.0)))
    return (drawn, spread)


def draw_keys(key, part):
    drawn, spread = shared_parts(key)
    return (drawn * spread).astype(jnp.bfloat16)


def draw_queries(key, part):
    key = jax.random.fold_in(key, 9)
    first = jax.random.fold_in(key, 0)
    third = jax.random.fold_in(key, 2)
    spread = jnp.exp(jax.random.uniform(first, (TOKENS, 1), jnp.float32, math.log(0.25), math.log(2.5)))
    drawn = jnp.clip(jax.random.normal(third, (TOKENS, QH * HD), jnp.float32), -6.0, 6.0)
    return (drawn * spread).astype(jnp.bfloat16)


def draw_doc_lengths(key, part):
    key = jax.random.fold_in(key, 13)
    first, second = jax.random.split(key, 2)
    rest = TOKENS - DOC_MAX
    cuts = jax.random.permutation(first, rest - 1)[:DOCS - 2].astype(jnp.int32) + 1
    cuts = jnp.sort(cuts)
    edges = jnp.concatenate([jnp.zeros((1,), jnp.int32), cuts, jnp.full((1,), rest, jnp.int32)])
    others = edges[1:] - edges[:-1]
    lengths = jnp.concatenate([jnp.full((1,), DOC_MAX, jnp.int32), others])
    place = jax.random.randint(second, (), 0, DOCS)
    return jnp.roll(lengths, place).astype(jnp.int32)


def block_levels(stream_key, shape, shards, low, top_value):
    factor_of = 1.0
    for axis_at, shards_of in shards:
        draws = jax.random.uniform(jax.random.fold_in(jax.random.fold_in(stream_key, 6), axis_at), (shards_of,), jnp.float32, low / len(shards), top_value / len(shards))
        factor_of = factor_of * jnp.repeat(jnp.exp(draws), shape[axis_at] // shards_of).reshape((-1,) + (1,) * (len(shape) - 1 - axis_at))
    return factor_of


def bell_draw(own_key, shape, scale, reach, cuts=(), held_as=jnp.bfloat16):
    factor_of = block_levels(own_key, shape, cuts, -0.22, 0.18) if cuts else 1.0
    drawn = jax.random.normal(own_key, shape, jnp.float32) * scale * factor_of
    return jnp.minimum(jnp.maximum(drawn, -reach), reach).astype(held_as)


def setup_inputs(seed: int = 0) -> dict:
    key_list = jax.random.split(jax.random.key(seed), 6)
    queries = draw_queries(jax.random.fold_in(key_list[5], 71), 0)
    keys = draw_keys(jax.random.fold_in(key_list[5], 71), 0)
    values = bell_draw(key_list[2], (TOKENS, KH * HD), 1.0, 6.0, ((0, 32), (1, 8)))
    grad_out = bell_draw(key_list[3], (TOKENS, QH * HD), 1.0, 6.0, ((0, 32), (1, 8)))
    doc_lengths = draw_doc_lengths(jax.random.fold_in(key_list[5], 71), 0)
    return dict(queries=queries, keys=keys, values=values, grad_out=grad_out, doc_lengths=doc_lengths)


def row_starts(doc_lengths, positions):
    ends = jnp.cumsum(doc_lengths)
    before = (ends[None, :] <= positions[:, None]).astype(jnp.int32)
    return jnp.sum(before * doc_lengths[None, :], axis=1)


def reference(queries, keys, values, grad_out, doc_lengths):
    scale = HD ** -0.5
    blocks = TOKENS // TOK_DEV
    span = DOC_MAX + TOK_DEV
    query_all = queries.reshape(TOKENS, KH, GROUP, HD)
    grad_all = grad_out.reshape(TOKENS, KH, GROUP, HD)
    padding = jnp.zeros((DOC_MAX, KH, HD), jnp.bfloat16)
    key_pad = jnp.concatenate([padding, keys.reshape(TOKENS, KH, HD)], axis=0)
    value_pad = jnp.concatenate([padding, values.reshape(TOKENS, KH, HD)], axis=0)

    def step(carry, block):
        key_acc, value_acc = carry
        first = block * TOK_DEV
        query_blk = lax.dynamic_slice_in_dim(query_all, first, TOK_DEV, 0).astype(jnp.float32)
        grad_blk = lax.dynamic_slice_in_dim(grad_all, first, TOK_DEV, 0).astype(jnp.float32)
        key_blk = lax.dynamic_slice_in_dim(key_pad, first, span, 0).astype(jnp.float32)
        value_blk = lax.dynamic_slice_in_dim(value_pad, first, span, 0).astype(jnp.float32)
        query_pos = first + jnp.arange(TOK_DEV, dtype=jnp.int32)
        key_pos = first - DOC_MAX + jnp.arange(span, dtype=jnp.int32)
        starts = row_starts(doc_lengths, query_pos)
        mask = (key_pos[None, :] >= starts[:, None]) & (key_pos[None, :] <= query_pos[:, None])
        scores = jnp.einsum("qhgd,khd->hgqk", query_blk, key_blk) * scale
        top = jnp.max(jnp.where(mask, scores, -jnp.inf), axis=-1)
        total = jnp.sum(jnp.where(mask, jnp.exp(scores - top[..., None]), 0.0), axis=-1)
        lse = top + jnp.log(total)
        probs = jnp.where(mask, jnp.exp(scores - lse[..., None]), 0.0)
        grad_probs = jnp.einsum("qhgd,khd->hgqk", grad_blk, value_blk)
        delta = jnp.sum(probs * grad_probs, axis=-1)
        grad_scores = probs * (grad_probs - delta[..., None])
        probs_b = lax.optimization_barrier(probs.astype(jnp.bfloat16)).astype(jnp.float32)
        grad_b = lax.optimization_barrier(grad_scores.astype(jnp.bfloat16)).astype(jnp.float32)
        grad_q = (jnp.einsum("hgqk,khd->qhgd", grad_b, key_blk) * scale).astype(jnp.bfloat16)
        key_add = jnp.einsum("hgqk,qhgd->khd", grad_b, query_blk) * scale
        value_add = jnp.einsum("hgqk,qhgd->khd", probs_b, grad_blk)
        key_acc = lax.dynamic_update_slice_in_dim(key_acc, lax.dynamic_slice_in_dim(key_acc, first, span, 0) + key_add, first, 0)
        value_acc = lax.dynamic_update_slice_in_dim(value_acc, lax.dynamic_slice_in_dim(value_acc, first, span, 0) + value_add, first, 0)
        return (key_acc, value_acc), grad_q

    empty = jnp.zeros((DOC_MAX + TOKENS, KH, HD), jnp.float32)
    (key_acc, value_acc), grad_blocks = lax.scan(step, (empty, empty), jnp.arange(blocks, dtype=jnp.int32))
    grad_queries = grad_blocks.reshape(TOKENS, QH * HD)
    grad_keys = key_acc[DOC_MAX:].reshape(TOKENS, KH * HD).astype(jnp.bfloat16)
    grad_values = value_acc[DOC_MAX:].reshape(TOKENS, KH * HD).astype(jnp.bfloat16)
    return grad_queries, grad_keys, grad_values
```

```python
import math

import jax
import jax.numpy as jnp
from jax import lax
from jax.experimental import pallas as pl
from jax.experimental.pallas import tpu as pltpu
from jax.sharding import Mesh, PartitionSpec as P

HD = 128
GROUP = 4
ROWS = 256
SLAB = 4
REACH = 5
HALF = 3
HERE = (0, 2)
THERE = (2, 4)
DOC_COUNT = 17
SCALE = HD ** -0.5
SCALE2 = SCALE * math.log2(math.e)
MASKED = -1e30
EMPTY = -1e29
VMEM_LIMIT = 16 * 1024 * 1024
NT = (((1,), (1,)), ((), ()))
NN = (((1,), (0,)), ((), ()))
F32 = jnp.float32
BF16 = jnp.bfloat16


def dot_nt(a, b):
    return lax.dot_general(a, b, NT, preferred_element_type=F32)


def dot_nn(a, b):
    return lax.dot_general(a, b, NN, preferred_element_type=F32)


def start_of(doc_ref, positions):
    end = jnp.int32(0)
    starts = jnp.zeros_like(positions)
    for doc in range(DOC_COUNT):
        length = doc_ref[doc]
        end = end + length
        starts = starts + jnp.where(end <= positions, length, 0)
    return starts


def tile_mask(doc_ref, query_block, key_block):
    positions = query_block * ROWS + lax.broadcasted_iota(jnp.int32, (1, ROWS), 1)
    starts = start_of(doc_ref, positions)
    key_pos = key_block * ROWS + lax.broadcasted_iota(jnp.int32, (ROWS, ROWS), 0)
    return (key_pos >= starts) & (key_pos <= positions)


def step_range(doc_ref, z, j, qb):
    first = start_of(doc_ref, (SLAB * z + qb) * ROWS) // ROWS
    low = jnp.maximum((first - j + SLAB - 1) >> 2, 0)
    return jnp.where(j <= qb, 0, 1), z - low


def pack_kernel(q_ref, g_ref, k_ref, v_ref, qg_ref, kv_ref, sems):
    wide, thin = GROUP * HD, HD
    copies = [
        pltpu.make_async_copy(k_ref, kv_ref.at[:, :thin], sems.at[0]),
        pltpu.make_async_copy(v_ref, kv_ref.at[:, thin:], sems.at[1]),
        pltpu.make_async_copy(q_ref, qg_ref.at[:, :wide], sems.at[2]),
        pltpu.make_async_copy(g_ref, qg_ref.at[:, wide:], sems.at[3]),
    ]
    for copy in copies:
        copy.start()
    for copy in copies:
        copy.wait()


def stats_steps(place_ref, doc_ref, rels, base, qg_all, kv_all, in_ref, out_ref):
    z, j = place_ref[0], place_ref[1]

    def per_block(rel, _):
        qb = j ^ rel
        low, high = step_range(doc_ref, z, j, qb)

        def per_step(k, carry):
            mask = tile_mask(doc_ref, SLAB * z + qb, SLAB * (z - k) + j)
            keys = kv_all[k, :, :HD]
            values = kv_all[k, :, HD:]
            new = []
            for h in range(GROUP):
                top, total, dot = carry[3 * h : 3 * h + 3]
                q = qg_all[rel, :, h * HD : (h + 1) * HD]
                g = qg_all[rel, :, (GROUP + h) * HD : (GROUP + h + 1) * HD]
                s = jnp.where(mask, dot_nt(keys, q) * SCALE2, MASKED)
                new_top = jnp.maximum(top, jnp.max(s, axis=0, keepdims=True))
                p = jnp.exp2(s - new_top)
                dp = dot_nt(values, g)
                factor = jnp.exp2(top - new_top)
                new += [
                    new_top,
                    total * factor + jnp.sum(p, axis=0, keepdims=True),
                    dot * factor + jnp.sum(p * dp, axis=0, keepdims=True),
                ]
            return tuple(new)

        if in_ref is None:
            zero = jnp.zeros((1, ROWS), F32)
            init = (jnp.full((1, ROWS), EMPTY, F32), zero, zero) * GROUP
        else:
            init = tuple(
                in_ref[part, pl.ds(qb * GROUP + h, 1), :]
                for h in range(GROUP)
                for part in range(3)
            )
        first, end = jnp.maximum(low, base), jnp.minimum(high + 1, base + HALF)
        done = lax.fori_loop(first, end, per_step, init)
        for h in range(GROUP):
            for part in range(3):
                out_ref[part, pl.ds(qb * GROUP + h, 1), :] = done[3 * h + part]
        return 0

    lax.fori_loop(rels[0], rels[1], per_block, 0)


def here_stats_kernel(place_ref, doc_ref, qg0, qg1, kv0, kv1, kv2, out_ref, kv_near, qg_here):
    for slot, ref in enumerate((qg0, qg1)):
        qg_here[slot] = ref[...]
    for slot, ref in enumerate((kv0, kv1, kv2)):
        kv_near[slot] = ref[...]
    stats_steps(place_ref, doc_ref, HERE, 0, qg_here, kv_near, None, out_ref)


def there_stats_kernel(place_ref, doc_ref, in_ref, kv_near, qg0, qg1, qg2, qg3, out_ref, qg_all):
    for slot, ref in enumerate((qg0, qg1, qg2, qg3)):
        qg_all[slot] = ref[...]
    out_ref[...] = in_ref[...]
    stats_steps(place_ref, doc_ref, THERE, 0, qg_all, kv_near, None, out_ref)


def far_stats_kernel(place_ref, doc_ref, in_ref, qg_all, kv_near, kv3, kv4, kv5, out_ref, kv_all):
    kv_all[:HALF] = kv_near[...]
    for slot, ref in enumerate((kv3, kv4, kv5)):
        kv_all[HALF + slot] = ref[...]
    stats_steps(place_ref, doc_ref, (0, SLAB), HALF, qg_all, kv_all, in_ref, out_ref)


def combine_stats(st_refs, lse_buf, delta_buf):
    stats = [ref[...] for ref in st_refs]
    top = jnp.maximum(
        jnp.maximum(stats[0][0], stats[1][0]), jnp.maximum(stats[2][0], stats[3][0])
    )
    total = jnp.zeros_like(top)
    dot = jnp.zeros_like(top)
    for st in stats:
        factor = jnp.exp2(st[0] - top)
        total = total + st[1] * factor
        dot = dot + st[2] * factor
    lse_buf[...] = top + jnp.log2(total)
    delta_buf[...] = dot / total


def visit_step(
    place_ref, doc_ref, k, rels, first, qg_all, kv_all, lse_buf, delta_buf, dqt, acc
):
    z, j = place_ref[0], place_ref[1]
    keys_t = kv_all[k, :, :HD].astype(F32).T.astype(BF16)

    def per_block(rel, _):
        qb = j ^ rel
        low, high = step_range(doc_ref, z, j, qb)

        @pl.when((k >= low) & (k <= high))
        def _():
            mask = tile_mask(doc_ref, SLAB * z + qb, SLAB * (z - k) + j)
            keys = kv_all[k, :, :HD]
            values = kv_all[k, :, HD:]
            dk = dv = None
            for h in range(GROUP):
                q = qg_all[rel, :, h * HD : (h + 1) * HD]
                g = qg_all[rel, :, (GROUP + h) * HD : (GROUP + h + 1) * HD]
                lse = lse_buf[pl.ds(qb * GROUP + h, 1), :]
                delta = delta_buf[pl.ds(qb * GROUP + h, 1), :]
                p = jnp.where(mask, jnp.exp2(dot_nt(keys, q) * SCALE2 - lse), 0.0)
                ds = p * (dot_nt(values, g) - delta)
                pb = p.astype(BF16)
                dsb = ds.astype(BF16)
                dv_add, dk_add = dot_nn(pb, g), dot_nn(dsb, q)
                dv = dv_add if dv is None else dv + dv_add
                dk = dk_add if dk is None else dk + dk_add
                dqt[(rel - first) * GROUP + h] += dot_nn(keys_t, dsb)
            acc[:, :HD] += dk
            acc[:, HD:] += dv

        return 0

    lax.fori_loop(rels[0], rels[1], per_block, 0)


def write_dq(dqt, slot, out_ref):
    for h in range(GROUP):
        dq = dqt[slot * GROUP + h].T * SCALE
        out_ref[:, h * HD : (h + 1) * HD] = dq.astype(BF16)


def write_dkv(out_ref, slot, acc):
    out_ref[slot, :, :HD] = (acc[:, :HD] * SCALE).astype(out_ref.dtype)
    out_ref[slot, :, HD:] = acc[:, HD:].astype(out_ref.dtype)


def far_kernel(
    place_ref, doc_ref, st0, st1, st2, st3, qg_all, kv_all,
    dqt_ref, dkv_ref, acc0_ref, lse_ref, delta_ref, acc,
):
    combine_stats((st0, st1, st2, st3), lse_ref, delta_ref)
    dqt_ref[...] = jnp.zeros_like(dqt_ref)

    def per_step(step, _):
        k = jnp.where(step == 0, 0, REACH + 1 - step)
        acc[...] = jnp.zeros_like(acc)
        visit_step(
            place_ref, doc_ref, k, (jnp.where(step == 0, THERE[0], 0), SLAB), 0,
            qg_all, kv_all, lse_ref, delta_ref, dqt_ref, acc,
        )

        @pl.when(step == 0)
        def _():
            acc0_ref[...] = acc[...]

        @pl.when(step > 0)
        def _():
            write_dkv(dkv_ref, k - HALF, acc)

        return 0

    lax.fori_loop(0, HALF + 1, per_step, 0)


def near_kernel(
    place_ref, doc_ref, lse_ref, delta_ref, qg_all, kv_all, dqt_in,
    dqt_out, keep_ref, send_ref, dkv_ref, dqt, acc,
):
    dqt[...] = dqt_in[...]

    def per_step(step, _):
        k = 2 - step
        acc[...] = jnp.zeros_like(acc)
        visit_step(
            place_ref, doc_ref, k, (0, SLAB), 0,
            qg_all, kv_all, lse_ref, delta_ref, dqt, acc,
        )
        write_dkv(dkv_ref, k - 1, acc)
        return 0

    lax.fori_loop(0, 2, per_step, 0)
    write_dq(dqt, 2, keep_ref)
    write_dq(dqt, 3, send_ref)
    dqt_out[...] = dqt[: 2 * GROUP]


def own_kernel(
    place_ref, doc_ref, lse_ref, delta_ref, qg_all, kv_all, dqt_in, acc0,
    keep_ref, send_ref, dkv_ref, dqt, acc,
):
    dqt[...] = dqt_in[...]
    acc[...] = acc0[...]
    visit_step(
        place_ref, doc_ref, jnp.int32(0), HERE, 0,
        qg_all, kv_all, lse_ref, delta_ref, dqt, acc,
    )
    write_dkv(dkv_ref, 0, acc)
    write_dq(dqt, 0, keep_ref)
    write_dq(dqt, 1, send_ref)


def pair_kernel(keep, got, out_ref):
    out_ref[...] = (keep[...].astype(F32) + got[...].astype(F32)).astype(BF16)


def merge_kernel(keep, beside, across, dkv0, got1, got2, got5, out_ref):
    parts, part = out_ref.shape[:2]
    width = GROUP * HD
    dq = keep[...].astype(F32) + beside[...].astype(F32) + across[...].astype(F32)
    dkv = dkv0[0] + got1[...].astype(F32) + got2[...].astype(F32) + got5[...].astype(F32)
    out_ref[:, :, :width] = dq.astype(BF16).reshape(parts, part, width)
    out_ref[:, :, width:] = dkv.astype(BF16).reshape(parts, part, 2 * HD)


def finish_kernel(got, q_ref, k_ref, v_ref):
    width = GROUP * HD
    for t in range(got.shape[0]):
        q_ref[:, t * width : (t + 1) * width] = got[t, :, :width]
        k_ref[:, t * HD : (t + 1) * HD] = got[t, :, width : width + HD]
        v_ref[:, t * HD : (t + 1) * HD] = got[t, :, width + HD :]


SMEM_SPEC = pl.BlockSpec(memory_space=pltpu.SMEM)
VMEM_SPEC = pl.BlockSpec(memory_space=pltpu.VMEM)


def call(kernel, name, outs, scratch, *args, scalars=2):
    return pl.pallas_call(
        kernel,
        out_shape=tuple(jax.ShapeDtypeStruct(shape, dtype) for shape, dtype in outs),
        in_specs=[SMEM_SPEC] * scalars + [VMEM_SPEC] * (len(args) - scalars),
        out_specs=(VMEM_SPEC,) * len(outs),
        scratch_shapes=[pltpu.VMEM(shape, dtype) for shape, dtype in scratch],
        compiler_params=pltpu.CompilerParams(vmem_limit_bytes=VMEM_LIMIT),
        cost_estimate=pl.CostEstimate(flops=1, bytes_accessed=1, transcendentals=0),
        name=name,
    )(*args)


QG_ALL = ((SLAB, ROWS, 2 * GROUP * HD), BF16)
QG_HERE = ((2, ROWS, 2 * GROUP * HD), BF16)
KV_ALL = ((REACH + 1, ROWS, 2 * HD), BF16)
KV_NEAR = ((HALF, ROWS, 2 * HD), BF16)
STATS = ((3, SLAB * GROUP, ROWS), F32)
ROW_STATS = ((SLAB * GROUP, ROWS), F32)
DQT = ((SLAB * GROUP, HD, ROWS), F32)
DQT_HALF = ((2 * GROUP, HD, ROWS), F32)
ACC = ((ROWS, 2 * HD), F32)
DQ = ((ROWS, GROUP * HD), BF16)


def flip(x, axis):
    return lax.ppermute(x, axis, [(0, 1), (1, 0)])


def shift(x, by, slabs):
    pairs = [(i, i + by) for i in range(slabs) if 0 <= i + by < slabs]
    return lax.ppermute(x, "z", pairs)


def shift_last(x, by, slabs):
    last = SLAB - 1
    pairs = [
        (i * SLAB + last, (i + by) * SLAB + last) for i in range(slabs) if 0 <= i + by < slabs
    ]
    return lax.ppermute(x, ("z", "y", "core"), pairs)


def local(queries, keys, values, grad_out, doc_lengths):
    z = lax.axis_index("z")
    j = lax.axis_index(("y", "core"))
    slabs = lax.axis_size("z")
    place = jnp.stack((z, j)).astype(jnp.int32)

    qg, kv = pl.pallas_call(
        pack_kernel,
        out_shape=(
            jax.ShapeDtypeStruct((ROWS, 2 * GROUP * HD), BF16),
            jax.ShapeDtypeStruct((ROWS, 2 * HD), BF16),
        ),
        in_specs=[pl.BlockSpec(memory_space=pltpu.HBM)] * 4,
        out_specs=(VMEM_SPEC,) * 2,
        scratch_shapes=[pltpu.SemaphoreType.DMA((4,))],
        compiler_params=pltpu.CompilerParams(vmem_limit_bytes=56 * 1024 * 1024),
        cost_estimate=pl.CostEstimate(flops=1, bytes_accessed=1, transcendentals=0),
        name="pack",
    )(queries, grad_out, keys, values)
    across = flip(qg, "y")
    kv1 = shift(kv, 1, slabs)
    kv2 = shift(kv, 2, slabs)
    beside = flip(qg, "core")
    kv5 = shift_last(kv, 5, slabs)
    kv2 = lax.optimization_barrier(kv2)
    kv3 = shift(kv2, 1, slabs)

    stats, kv_near = call(
        here_stats_kernel, "here_statistics", [STATS, KV_NEAR], [QG_HERE],
        place, doc_lengths, qg, beside, kv, kv1, kv2,
    )
    across, stats, kv3, kv5 = lax.optimization_barrier((across, stats, kv3, kv5))
    kv4 = shift(kv3, 1, slabs)
    both = flip(across, "core")
    stats, qg_all = call(
        there_stats_kernel, "there_statistics", [STATS, QG_ALL], [],
        place, doc_lengths, stats, kv_near, qg, beside, across, both,
    )
    stats, kv_all = call(
        far_stats_kernel, "far_statistics", [STATS, KV_ALL], [],
        place, doc_lengths, stats, qg_all, kv_near, kv3, kv4, kv5,
    )
    stats_y = flip(stats, "y")
    stats_c = flip(stats, "core")
    stats_yc = flip(stats_y, "core")

    dqt, dkv_far, acc0, lse, delta = call(
        far_kernel, "far_gradients",
        [DQT, ((HALF,) + ACC[0], BF16), ACC, ROW_STATS, ROW_STATS], [ACC],
        place, doc_lengths, stats, stats_c, stats_y, stats_yc, qg_all, kv_all,
    )
    got_far = shift(dkv_far[:2], -2, slabs)
    got5 = shift_last(dkv_far[2], -5, slabs)
    dqt, there_keep, there_send, dkv_near = call(
        near_kernel, "near_gradients",
        [DQT_HALF, DQ, DQ, ((2,) + ACC[0], F32)], [DQT, ACC],
        place, doc_lengths, lse, delta, qg_all, kv_all, dqt,
    )
    there_got = flip(there_send, "core")
    dkv_send = (dkv_near + got_far.astype(F32)).astype(BF16)
    dq_pair, = call(pair_kernel, "pair", [DQ], [], there_keep, there_got, scalars=0)
    dkv_send, dq_pair, dqt = lax.optimization_barrier((dkv_send, dq_pair, dqt))
    got2 = shift(dkv_send[1], -2, slabs)
    got1 = shift(dkv_send[0], -1, slabs)
    dq_across = flip(dq_pair, "y")
    dq_keep, dq_send, dkv0 = call(
        own_kernel, "own_gradients",
        [DQ, DQ, ((1,) + ACC[0], F32)], [DQT_HALF, ACC],
        place, doc_lengths, lse, delta, qg_all, kv_all, dqt, acc0,
    )
    dq_send, dq_across, got1, got2, got5 = lax.optimization_barrier(
        (dq_send, dq_across, got1, got2, got5)
    )
    dq_beside = flip(dq_send, "core")

    tp = lax.axis_size("tp")
    part = ROWS // tp
    width = GROUP * HD
    whole, = call(
        merge_kernel, "merge", [((tp, part, width + 2 * HD), BF16)], [],
        dq_keep, dq_beside, dq_across, dkv0, got1, got2, got5, scalars=0,
    )
    got = lax.all_to_all(whole, "tp", split_axis=0, concat_axis=0, tiled=True)
    return call(
        finish_kernel, "finish",
        [((part, tp * width), BF16), ((part, tp * HD), BF16), ((part, tp * HD), BF16)], [],
        got, scalars=0,
    )


def solution(mesh):
    tp = mesh.shape["tp"]
    inner = Mesh(mesh.devices.reshape(-1, 2, 2, tp), ("z", "y", "core", "tp"))
    tokens = ("z", "y", "core")
    in_specs = (P(tokens, "tp"),) * 4 + (P(),)
    out_specs = (P(tokens + ("tp",), None),) * 3
    return jax.shard_map(local, mesh=inner, in_specs=in_specs, out_specs=out_specs, check_vma=False)
```

```python
import math

import jax
import jax.numpy as jnp
from jax import lax
from jax.experimental import pallas as pl
from jax.experimental.pallas import tpu as pltpu
from jax.sharding import Mesh, PartitionSpec as P

HD = 128
GROUP = 4
ROWS = 256
SLAB = 4
REACH = 5
HALF = 3
HERE = (0, 2)
THERE = (2, 4)
DOC_COUNT = 17
SCALE = HD ** -0.5
SCALE2 = SCALE * math.log2(math.e)
MASKED = -1e30
EMPTY = -1e29
VMEM_LIMIT = 16 * 1024 * 1024
NT = (((1,), (1,)), ((), ()))
NN = (((1,), (0,)), ((), ()))
F32 = jnp.float32
BF16 = jnp.bfloat16


def dot_nt(a, b):
    return lax.dot_general(a, b, NT, preferred_element_type=F32)


def dot_nn(a, b):
    return lax.dot_general(a, b, NN, preferred_element_type=F32)


def start_of(doc_ref, positions):
    end = jnp.int32(0)
    starts = jnp.zeros_like(positions)
    for doc in range(DOC_COUNT):
        length = doc_ref[doc]
        end = end + length
        starts = starts + jnp.where(end <= positions, length, 0)
    return starts


def step_ranges(place_ref, doc_ref, steps_ref):
    z, j = place_ref[0], place_ref[1]
    for rel in range(SLAB):
        qb = j ^ rel
        first = start_of(doc_ref, (SLAB * z + qb) * ROWS) // ROWS
        steps_ref[2 * rel] = jnp.where(j <= qb, 0, 1)
        steps_ref[2 * rel + 1] = z - jnp.maximum((first - j + SLAB - 1) >> 2, 0)


def pack_kernel(q_ref, g_ref, k_ref, v_ref, qg_ref, kv_ref, sems):
    wide, thin = GROUP * HD, HD
    copies = [
        pltpu.make_async_copy(k_ref, kv_ref.at[:, :thin], sems.at[0]),
        pltpu.make_async_copy(v_ref, kv_ref.at[:, thin:], sems.at[1]),
        pltpu.make_async_copy(q_ref, qg_ref.at[:, :wide], sems.at[2]),
        pltpu.make_async_copy(g_ref, qg_ref.at[:, wide:], sems.at[3]),
    ]
    for copy in copies:
        copy.start()
    for copy in copies:
        copy.wait()


def stats_steps(place_ref, doc_ref, rels, steps, fresh, qg, kv, tops, weights, out_ref, ranges):
    z, j = place_ref[0], place_ref[1]
    step_ranges(place_ref, doc_ref, ranges)

    def per_block(rel, _):
        qb = j ^ rel
        positions = (SLAB * z + qb) * ROWS + lax.broadcasted_iota(jnp.int32, (1, ROWS), 1)
        starts = start_of(doc_ref, positions)

        def per_step(k, carry):
            key_pos = lax.broadcasted_iota(jnp.int32, (ROWS, ROWS), 0)
            offset = (SLAB * (z - k) + j) * ROWS
            mask = (key_pos >= starts - offset) & (key_pos <= positions - offset)
            keys = kv[k, :, :HD]
            values = kv[k, :, HD:]

            def products(h):
                q = qg[rel, :, h * HD : (h + 1) * HD]
                g = qg[rel, :, (GROUP + h) * HD : (GROUP + h + 1) * HD]
                return dot_nt(keys, q), dot_nt(values, g)

            new = []
            ahead = products(0)
            for h in range(GROUP):
                s, dp = ahead
                if h + 1 < GROUP:
                    ahead = products(h + 1)
                top, total, dot = carry[3 * h : 3 * h + 3]
                s = jnp.where(mask, s * SCALE2, MASKED)
                new_top = jnp.maximum(top, jnp.max(s, axis=0, keepdims=True))
                p = jnp.exp2(s - new_top)
                weights[rel * (REACH + 1) + k, h] = p.astype(BF16)
                tops[k, pl.ds(rel * GROUP + h, 1), :] = new_top
                factor = jnp.exp2(top - new_top)
                new += [
                    new_top,
                    total * factor + jnp.sum(p, axis=0, keepdims=True),
                    dot * factor + jnp.sum(p * dp, axis=0, keepdims=True),
                ]
            return tuple(new)

        if fresh:
            zero = jnp.zeros((1, ROWS), F32)
            init = (jnp.full((1, ROWS), EMPTY, F32), zero, zero) * GROUP
        else:
            init = tuple(
                out_ref[part, pl.ds(qb * GROUP + h, 1), :]
                for h in range(GROUP)
                for part in range(3)
            )
        first = jnp.maximum(ranges[2 * rel], steps[0])
        end = jnp.minimum(ranges[2 * rel + 1] + 1, steps[1])
        done = lax.fori_loop(first, end, per_step, init)
        for h in range(GROUP):
            for part in range(3):
                out_ref[part, pl.ds(qb * GROUP + h, 1), :] = done[3 * h + part]
        return 0

    lax.fori_loop(rels[0], rels[1], per_block, 0)


def first_stats_kernel(
    place_ref, doc_ref, qg0, qg1, kv0, out_ref, tops, weights, qg_all, kv_all, ranges
):
    qg_all[0] = qg0[...]
    qg_all[1] = qg1[...]
    kv_all[0] = kv0[...]
    stats_steps(
        place_ref, doc_ref, HERE, (0, 1), True, qg_all, kv_all, tops, weights, out_ref, ranges
    )


def here_stats_kernel(
    place_ref, doc_ref, in0, in1, in2, in3, qg_all, kv1, kv2, out_ref, tops, weights, kv_all, ranges
):
    del in0, in1, in2, in3
    kv_all[1] = kv1[...]
    kv_all[2] = kv2[...]
    stats_steps(
        place_ref, doc_ref, HERE, (1, HALF), False, qg_all, kv_all, tops, weights, out_ref, ranges
    )


def there_stats_kernel(
    place_ref, doc_ref, in0, in1, in2, in3, kv_all, qg2, qg3, out_ref, tops, weights, qg_all, ranges
):
    del in0, in1, in2, in3
    qg_all[2] = qg2[...]
    qg_all[3] = qg3[...]
    stats_steps(
        place_ref, doc_ref, THERE, (0, HALF), True, qg_all, kv_all, tops, weights, out_ref, ranges
    )


def far_stats_kernel(
    place_ref, doc_ref, in0, in1, in2, in3, qg_all, kv3, kv4, kv5,
    out_ref, tops, weights, kv_all, ranges,
):
    del in0, in1, in2, in3
    for slot, ref in enumerate((kv3, kv4, kv5)):
        kv_all[HALF + slot] = ref[...]
    stats_steps(
        place_ref, doc_ref, (0, SLAB), (HALF, REACH + 1), False,
        qg_all, kv_all, tops, weights, out_ref, ranges,
    )


def combine_stats(st_refs, lse_buf, delta_buf):
    stats = [ref[...] for ref in st_refs]
    top = jnp.maximum(
        jnp.maximum(stats[0][0], stats[1][0]), jnp.maximum(stats[2][0], stats[3][0])
    )
    total = jnp.zeros_like(top)
    dot = jnp.zeros_like(top)
    for st in stats:
        factor = jnp.exp2(st[0] - top)
        total = total + st[1] * factor
        dot = dot + st[2] * factor
    lse_buf[...] = top + jnp.log2(total)
    delta_buf[...] = dot / total


def visit_step(j, k, rels, ranges, data, dqt, acc):
    lse_buf, delta_buf, tops, weights, qg_all, kv_all = data
    keys_t = kv_all[k, :, :HD].astype(F32).T.astype(BF16)

    def per_block(rel, _):
        qb = j ^ rel

        @pl.when((k >= ranges[2 * rel]) & (k <= ranges[2 * rel + 1]))
        def _():
            values = kv_all[k, :, HD:]

            def grad_of(h):
                return qg_all[rel, :, (GROUP + h) * HD : (GROUP + h + 1) * HD]

            dk = dv = None
            ahead = dot_nt(values, grad_of(0))
            for h in range(GROUP):
                dp = ahead
                if h + 1 < GROUP:
                    ahead = dot_nt(values, grad_of(h + 1))
                q = qg_all[rel, :, h * HD : (h + 1) * HD]
                lse = lse_buf[pl.ds(qb * GROUP + h, 1), :]
                delta = delta_buf[pl.ds(qb * GROUP + h, 1), :]
                factor = jnp.exp2(tops[k, pl.ds(rel * GROUP + h, 1), :] - lse)
                p = weights[rel * (REACH + 1) + k, h].astype(F32) * factor
                ds = p * (dp - delta)
                pb = p.astype(BF16)
                dsb = ds.astype(BF16)
                dv_add, dk_add = dot_nn(pb, grad_of(h)), dot_nn(dsb, q)
                dv = dv_add if dv is None else dv + dv_add
                dk = dk_add if dk is None else dk + dk_add
                dqt[rel * GROUP + h] += dot_nn(keys_t, dsb)
            acc[:, :HD] += dk
            acc[:, HD:] += dv

        return 0

    lax.fori_loop(rels[0], rels[1], per_block, 0)


def write_dq(dqt, slot, out_ref):
    for h in range(GROUP):
        dq = dqt[slot * GROUP + h].T * SCALE
        out_ref[:, h * HD : (h + 1) * HD] = dq.astype(BF16)


def write_dkv(out_ref, acc):
    out_ref[:, :HD] = (acc[:, :HD] * SCALE).astype(out_ref.dtype)
    out_ref[:, HD:] = acc[:, HD:].astype(out_ref.dtype)


def far_kernel(
    place_ref, doc_ref, st0, st1, st2, st3, tops, weights, qg_all, kv_all,
    dqt, dkv34, dkv5, acc0_ref, lse_ref, delta_ref, acc, ranges,
):
    step_ranges(place_ref, doc_ref, ranges)
    combine_stats((st0, st1, st2, st3), lse_ref, delta_ref)
    dqt[...] = jnp.zeros_like(dqt)

    def per_step(step, _):
        k = jnp.where(step == 0, 0, REACH + 1 - step)
        acc[...] = jnp.zeros_like(acc)
        visit_step(
            place_ref[1], k, (jnp.where(step == 0, THERE[0], 0), SLAB), ranges,
            (lse_ref, delta_ref, tops, weights, qg_all, kv_all), dqt, acc,
        )

        @pl.when(step == 0)
        def _():
            acc0_ref[...] = acc[...]

        for slot, ref in enumerate((dkv5, dkv34.at[1], dkv34.at[0])):

            @pl.when(step == slot + 1)
            def _():
                write_dkv(ref, acc)

        return 0

    lax.fori_loop(0, HALF + 1, per_step, 0)


def near_kernel(
    place_ref, doc_ref, dqt_in, lse_ref, delta_ref, tops, weights, qg_all, kv_all,
    dqt, there_ref, dkv1, dkv2, acc, ranges,
):
    del dqt_in
    step_ranges(place_ref, doc_ref, ranges)

    def per_step(step, _):
        k = 2 - step
        acc[...] = jnp.zeros_like(acc)
        visit_step(
            place_ref[1], k, (0, SLAB), ranges,
            (lse_ref, delta_ref, tops, weights, qg_all, kv_all), dqt, acc,
        )

        @pl.when(k == 2)
        def _():
            write_dkv(dkv2, acc)

        @pl.when(k == 1)
        def _():
            write_dkv(dkv1, acc)

        return 0

    lax.fori_loop(0, 2, per_step, 0)
    write_dq(dqt, 2, there_ref.at[0])
    write_dq(dqt, 3, there_ref.at[1])


def own_kernel(
    place_ref, doc_ref, dqt_in, lse_ref, delta_ref, tops, weights, qg_all, kv_all, acc0,
    dqt, keep_ref, send_ref, dkv_ref, acc, ranges,
):
    del dqt_in
    step_ranges(place_ref, doc_ref, ranges)
    acc[...] = acc0[...]
    visit_step(
        place_ref[1], jnp.int32(0), HERE, ranges,
        (lse_ref, delta_ref, tops, weights, qg_all, kv_all), dqt, acc,
    )
    write_dkv(dkv_ref, acc)
    write_dq(dqt, 0, keep_ref)
    write_dq(dqt, 1, send_ref)


def merge_kernel(keep, beside, across, both, dkv0, got1, got2, got5, out_ref):
    parts, part = out_ref.shape[:2]
    width = GROUP * HD
    dq = keep[...].astype(F32) + beside[...].astype(F32)
    dq = dq + across[0].astype(F32) + both[...].astype(F32)
    dkv = dkv0[...] + got1[...].astype(F32) + got2[...].astype(F32) + got5[...].astype(F32)
    out_ref[:, :, :width] = dq.astype(BF16).reshape(parts, part, width)
    out_ref[:, :, width:] = dkv.astype(BF16).reshape(parts, part, 2 * HD)


def finish_kernel(got, q_ref, k_ref, v_ref):
    width = GROUP * HD
    for t in range(got.shape[0]):
        q_ref[:, t * width : (t + 1) * width] = got[t, :, :width]
        k_ref[:, t * HD : (t + 1) * HD] = got[t, :, width : width + HD]
        v_ref[:, t * HD : (t + 1) * HD] = got[t, :, width + HD :]


SMEM_SPEC = pl.BlockSpec(memory_space=pltpu.SMEM)
VMEM_SPEC = pl.BlockSpec(memory_space=pltpu.VMEM)


def call(kernel, name, outs, scratch, *args, scalars=2, aliases=None, ranges=True):
    return pl.pallas_call(
        kernel,
        out_shape=tuple(jax.ShapeDtypeStruct(shape, dtype) for shape, dtype in outs),
        in_specs=[SMEM_SPEC] * scalars + [VMEM_SPEC] * (len(args) - scalars),
        out_specs=(VMEM_SPEC,) * len(outs),
        scratch_shapes=[pltpu.VMEM(shape, dtype) for shape, dtype in scratch]
        + [pltpu.SMEM((2 * SLAB,), jnp.int32)] * ranges,
        input_output_aliases=aliases or {},
        compiler_params=pltpu.CompilerParams(vmem_limit_bytes=VMEM_LIMIT),
        cost_estimate=pl.CostEstimate(flops=1, bytes_accessed=1, transcendentals=0),
        name=name,
    )(*args)


QG_ALL = ((SLAB, ROWS, 2 * GROUP * HD), BF16)
KV_ALL = ((REACH + 1, ROWS, 2 * HD), BF16)
STATS = ((3, SLAB * GROUP, ROWS), F32)
TOPS = ((REACH + 1, SLAB * GROUP, ROWS), F32)
WEIGHTS = ((SLAB * (REACH + 1), GROUP, ROWS, ROWS), BF16)
ROW_STATS = ((SLAB * GROUP, ROWS), F32)
DQT = ((SLAB * GROUP, HD, ROWS), F32)
ACC = ((ROWS, 2 * HD), F32)
DKV = ((ROWS, 2 * HD), BF16)
DQ = ((ROWS, GROUP * HD), BF16)


def flip(x, axis):
    return lax.ppermute(x, axis, [(0, 1), (1, 0)])


def shift(x, by, slabs):
    pairs = [(i, i + by) for i in range(slabs) if 0 <= i + by < slabs]
    return lax.ppermute(x, "z", pairs)


def shift_last(x, by, slabs):
    last = SLAB - 1
    pairs = [
        (i * SLAB + last, (i + by) * SLAB + last) for i in range(slabs) if 0 <= i + by < slabs
    ]
    return lax.ppermute(x, ("z", "y", "core"), pairs)


def local(queries, keys, values, grad_out, doc_lengths):
    z = lax.axis_index("z")
    j = lax.axis_index(("y", "core"))
    slabs = lax.axis_size("z")
    place = jnp.stack((z, j)).astype(jnp.int32)

    qg, kv = pl.pallas_call(
        pack_kernel,
        out_shape=(
            jax.ShapeDtypeStruct((ROWS, 2 * GROUP * HD), BF16),
            jax.ShapeDtypeStruct((ROWS, 2 * HD), BF16),
        ),
        in_specs=[pl.BlockSpec(memory_space=pltpu.HBM)] * 4,
        out_specs=(VMEM_SPEC,) * 2,
        scratch_shapes=[pltpu.SemaphoreType.DMA((4,))],
        compiler_params=pltpu.CompilerParams(vmem_limit_bytes=56 * 1024 * 1024),
        cost_estimate=pl.CostEstimate(flops=1, bytes_accessed=1, transcendentals=0),
        name="pack",
    )(queries, grad_out, keys, values)
    across = flip(qg, "y")
    kv1 = shift(kv, 1, slabs)
    kv2 = shift(kv, 2, slabs)
    beside = flip(qg, "core")
    kv5 = shift_last(kv, 5, slabs)

    stats, tops, weights, qg_all, kv_all = call(
        first_stats_kernel, "first_statistics", [STATS, TOPS, WEIGHTS, QG_ALL, KV_ALL], [],
        place, doc_lengths, qg, beside, kv,
    )
    kv2, stats = lax.optimization_barrier((kv2, stats))
    kv3 = shift(kv2, 1, slabs)
    stats, tops, weights, kv_all = call(
        here_stats_kernel, "here_statistics", [STATS, TOPS, WEIGHTS, KV_ALL], [],
        place, doc_lengths, stats, tops, weights, kv_all, qg_all, kv1, kv2,
        aliases={2: 0, 3: 1, 4: 2, 5: 3},
    )
    across, stats, kv3, kv5 = lax.optimization_barrier((across, stats, kv3, kv5))
    kv4 = shift(kv3, 1, slabs)
    both = flip(across, "core")
    stats, tops, weights, qg_all = call(
        there_stats_kernel, "there_statistics", [STATS, TOPS, WEIGHTS, QG_ALL], [],
        place, doc_lengths, stats, tops, weights, qg_all, kv_all, across, both,
        aliases={2: 0, 3: 1, 4: 2, 5: 3},
    )
    stats, tops, weights, kv_all = call(
        far_stats_kernel, "far_statistics", [STATS, TOPS, WEIGHTS, KV_ALL], [],
        place, doc_lengths, stats, tops, weights, kv_all, qg_all, kv3, kv4, kv5,
        aliases={2: 0, 3: 1, 4: 2, 5: 3},
    )
    stats_y = flip(stats, "y")
    stats_c = flip(stats, "core")
    stats_yc = flip(stats_y, "core")

    data = (tops, weights, qg_all, kv_all)
    dqt, dkv34, dkv5, acc0, lse, delta = call(
        far_kernel, "far_gradients",
        [DQT, ((2,) + DKV[0], BF16), DKV, ACC, ROW_STATS, ROW_STATS], [ACC],
        place, doc_lengths, stats, stats_c, stats_y, stats_yc, *data,
    )
    got_far = shift(dkv34, -2, slabs)
    got5 = shift_last(dkv5, -5, slabs)
    dqt, there, dkv1, dkv2 = call(
        near_kernel, "near_gradients", [DQT, ((2,) + DQ[0], BF16), ACC, ACC], [ACC],
        place, doc_lengths, dqt, lse, delta, *data, aliases={2: 0},
    )
    dq_across = flip(there, "y")
    dkv1 = (dkv1 + got_far[0].astype(F32)).astype(BF16)
    dkv2 = (dkv2 + got_far[1].astype(F32)).astype(BF16)
    got2 = shift(dkv2, -2, slabs)
    got1 = shift(dkv1, -1, slabs)
    _, dq_keep, dq_send, dkv0 = call(
        own_kernel, "own_gradients", [DQT, DQ, DQ, ACC], [ACC],
        place, doc_lengths, dqt, lse, delta, *data, acc0, aliases={2: 0},
    )
    dq_beside = flip(dq_send, "core")
    dq_across, got1, got2, got5 = lax.optimization_barrier((dq_across, got1, got2, got5))
    dq_both = flip(dq_across[1], "core")

    tp = lax.axis_size("tp")
    part = ROWS // tp
    width = GROUP * HD
    whole, = call(
        merge_kernel, "merge", [((tp, part, width + 2 * HD), BF16)], [],
        dq_keep, dq_beside, dq_across, dq_both, dkv0, got1, got2, got5, scalars=0, ranges=False,
    )
    got = lax.all_to_all(whole, "tp", split_axis=0, concat_axis=0, tiled=True)
    return call(
        finish_kernel, "finish",
        [((part, tp * width), BF16), ((part, tp * HD), BF16), ((part, tp * HD), BF16)], [],
        got, scalars=0, ranges=False,
    )


def solution(mesh):
    tp = mesh.shape["tp"]
    inner = Mesh(mesh.devices.reshape(-1, 2, 2, tp), ("z", "y", "core", "tp"))
    tokens = ("z", "y", "core")
    in_specs = (P(tokens, "tp"),) * 4 + (P(),)
    out_specs = (P(tokens + ("tp",), None),) * 3
    return jax.shard_map(local, mesh=inner, in_specs=in_specs, out_specs=out_specs, check_vma=False)
```

```python
import math

import jax
import jax.numpy as jnp
from jax import lax
from jax.experimental import pallas as pl
from jax.experimental.pallas import tpu as pltpu
from jax.sharding import Mesh, PartitionSpec as P

HD = 128
GROUP = 4
ROWS = 256
SLAB = 4
REACH = 5
HALF = 3
HERE = (0, 2)
THERE = (2, 4)
DOC_COUNT = 17
SCALE = HD ** -0.5
SCALE2 = SCALE * math.log2(math.e)
MASKED = -1e30
EMPTY = -1e29
VMEM_LIMIT = 16 * 1024 * 1024
NT = (((1,), (1,)), ((), ()))
NN = (((1,), (0,)), ((), ()))
F32 = jnp.float32
BF16 = jnp.bfloat16


def dot_nt(a, b):
    return lax.dot_general(a, b, NT, preferred_element_type=F32)


def dot_nn(a, b):
    return lax.dot_general(a, b, NN, preferred_element_type=F32)


def start_of(doc_ref, positions):
    end = jnp.int32(0)
    starts = jnp.zeros_like(positions)
    for doc in range(DOC_COUNT):
        length = doc_ref[doc]
        end = end + length
        starts = starts + jnp.where(end <= positions, length, 0)
    return starts


def step_ranges(place_ref, doc_ref, steps_ref):
    z, j = place_ref[0], place_ref[1]
    for rel in range(SLAB):
        qb = j ^ rel
        first = start_of(doc_ref, (SLAB * z + qb) * ROWS) // ROWS
        steps_ref[2 * rel] = jnp.where(j <= qb, 0, 1)
        steps_ref[2 * rel + 1] = z - jnp.maximum((first - j + SLAB - 1) >> 2, 0)


def pack_kernel(q_ref, g_ref, k_ref, v_ref, qg_ref, kv_ref, sems):
    wide, thin = GROUP * HD, HD
    copies = [
        pltpu.make_async_copy(k_ref, kv_ref.at[:, :thin], sems.at[0]),
        pltpu.make_async_copy(v_ref, kv_ref.at[:, thin:], sems.at[1]),
        pltpu.make_async_copy(q_ref, qg_ref.at[:, :wide], sems.at[2]),
        pltpu.make_async_copy(g_ref, qg_ref.at[:, wide:], sems.at[3]),
    ]
    for copy in copies:
        copy.start()
    for copy in copies:
        copy.wait()


def stats_steps(place_ref, doc_ref, rels, steps, fresh, qg, kv, tops, weights, out_ref, ranges):
    z, j = place_ref[0], place_ref[1]
    step_ranges(place_ref, doc_ref, ranges)

    def per_block(rel, _):
        qb = j ^ rel
        positions = (SLAB * z + qb) * ROWS + lax.broadcasted_iota(jnp.int32, (1, ROWS), 1)
        starts = start_of(doc_ref, positions)

        def per_step(k, carry):
            key_pos = lax.broadcasted_iota(jnp.int32, (ROWS, ROWS), 0)
            offset = (SLAB * (z - k) + j) * ROWS
            mask = (key_pos >= starts - offset) & (key_pos <= positions - offset)
            keys = kv[k, :, :HD]
            values = kv[k, :, HD:]

            def products(h):
                q = qg[rel, :, h * HD : (h + 1) * HD]
                g = qg[rel, :, (GROUP + h) * HD : (GROUP + h + 1) * HD]
                return dot_nt(keys, q), dot_nt(values, g)

            new = []
            ahead = products(0)
            for h in range(GROUP):
                s, dp = ahead
                if h + 1 < GROUP:
                    ahead = products(h + 1)
                top, total, dot = carry[3 * h : 3 * h + 3]
                s = jnp.where(mask, s * SCALE2, MASKED)
                new_top = jnp.maximum(top, jnp.max(s, axis=0, keepdims=True))
                p = jnp.exp2(s - new_top)
                weights[rel * (REACH + 1) + k, h] = p.astype(BF16)
                tops[k, pl.ds(rel * GROUP + h, 1), :] = new_top
                factor = jnp.exp2(top - new_top)
                new += [
                    new_top,
                    total * factor + jnp.sum(p, axis=0, keepdims=True),
                    dot * factor + jnp.sum(p * dp, axis=0, keepdims=True),
                ]
            return tuple(new)

        if fresh:
            zero = jnp.zeros((1, ROWS), F32)
            init = (jnp.full((1, ROWS), EMPTY, F32), zero, zero) * GROUP
        else:
            init = tuple(
                out_ref[part, pl.ds(qb * GROUP + h, 1), :]
                for h in range(GROUP)
                for part in range(3)
            )
        first = jnp.maximum(ranges[2 * rel], steps[0])
        end = jnp.minimum(ranges[2 * rel + 1] + 1, steps[1])
        done = lax.fori_loop(first, end, per_step, init)
        for h in range(GROUP):
            for part in range(3):
                out_ref[part, pl.ds(qb * GROUP + h, 1), :] = done[3 * h + part]
        return 0

    lax.fori_loop(rels[0], rels[1], per_block, 0)


def first_stats_kernel(
    place_ref, doc_ref, qg0, qg1, kv0, out_ref, tops, weights, qg_all, kv_all, ranges
):
    qg_all[0] = qg0[...]
    qg_all[1] = qg1[...]
    kv_all[0] = kv0[...]
    stats_steps(
        place_ref, doc_ref, HERE, (0, 1), True, qg_all, kv_all, tops, weights, out_ref, ranges
    )


def here_stats_kernel(
    place_ref, doc_ref, in0, in1, in2, in3, qg_all, kv1, kv2, out_ref, tops, weights, kv_all, ranges
):
    del in0, in1, in2, in3
    kv_all[1] = kv1[...]
    kv_all[2] = kv2[...]
    stats_steps(
        place_ref, doc_ref, HERE, (1, HALF), False, qg_all, kv_all, tops, weights, out_ref, ranges
    )


def there_stats_kernel(
    place_ref, doc_ref, in0, in1, in2, in3, kv_all, qg2, qg3, out_ref, tops, weights, qg_all, ranges
):
    del in0, in1, in2, in3
    qg_all[2] = qg2[...]
    qg_all[3] = qg3[...]
    stats_steps(
        place_ref, doc_ref, THERE, (0, HALF), True, qg_all, kv_all, tops, weights, out_ref, ranges
    )


def far_stats_kernel(
    place_ref, doc_ref, in0, in1, in2, in3, qg_all, kv3, kv4, kv5,
    out_ref, tops, weights, kv_all, ranges,
):
    del in0, in1, in2, in3
    for slot, ref in enumerate((kv3, kv4, kv5)):
        kv_all[HALF + slot] = ref[...]
    stats_steps(
        place_ref, doc_ref, (0, SLAB), (HALF, REACH + 1), False,
        qg_all, kv_all, tops, weights, out_ref, ranges,
    )


def combine_stats(st_refs, lse_buf, delta_buf):
    stats = [ref[...] for ref in st_refs]
    top = jnp.maximum(
        jnp.maximum(stats[0][0], stats[1][0]), jnp.maximum(stats[2][0], stats[3][0])
    )
    total = jnp.zeros_like(top)
    dot = jnp.zeros_like(top)
    for st in stats:
        factor = jnp.exp2(st[0] - top)
        total = total + st[1] * factor
        dot = dot + st[2] * factor
    lse_buf[...] = top + jnp.log2(total)
    delta_buf[...] = dot / total


def visit_step(j, k, rels, ranges, data, dqt, acc):
    lse_buf, delta_buf, tops, weights, qg_all, kv_all = data
    keys_t = kv_all[k, :, :HD].astype(F32).T.astype(BF16)

    def per_block(rel, _):
        qb = j ^ rel

        @pl.when((k >= ranges[2 * rel]) & (k <= ranges[2 * rel + 1]))
        def _():
            values = kv_all[k, :, HD:]

            def grad_of(h):
                return qg_all[rel, :, (GROUP + h) * HD : (GROUP + h + 1) * HD]

            dk = dv = None
            ahead = dot_nt(values, grad_of(0))
            for h in range(GROUP):
                dp = ahead
                if h + 1 < GROUP:
                    ahead = dot_nt(values, grad_of(h + 1))
                q = qg_all[rel, :, h * HD : (h + 1) * HD]
                lse = lse_buf[pl.ds(qb * GROUP + h, 1), :]
                delta = delta_buf[pl.ds(qb * GROUP + h, 1), :]
                factor = jnp.exp2(tops[k, pl.ds(rel * GROUP + h, 1), :] - lse)
                p = weights[rel * (REACH + 1) + k, h].astype(F32) * factor
                ds = p * (dp - delta)
                pb = p.astype(BF16)
                dsb = ds.astype(BF16)
                dv_add, dk_add = dot_nn(pb, grad_of(h)), dot_nn(dsb, q)
                dv = dv_add if dv is None else dv + dv_add
                dk = dk_add if dk is None else dk + dk_add
                dqt[rel * GROUP + h] += dot_nn(keys_t, dsb)
            acc[:, :HD] += dk
            acc[:, HD:] += dv

        return 0

    lax.fori_loop(rels[0], rels[1], per_block, 0)


def write_dq(dqt, slot, out_ref):
    for h in range(GROUP):
        dq = dqt[slot * GROUP + h].T * SCALE
        out_ref[:, h * HD : (h + 1) * HD] = dq.astype(BF16)


def write_dkv(out_ref, acc):
    out_ref[:, :HD] = (acc[:, :HD] * SCALE).astype(out_ref.dtype)
    out_ref[:, HD:] = acc[:, HD:].astype(out_ref.dtype)


def far_kernel(
    place_ref, doc_ref, st0, st1, st2, st3, tops, weights, qg_all, kv_all,
    dqt, dkv34, dkv5, acc0_ref, lse_ref, delta_ref, acc, ranges,
):
    step_ranges(place_ref, doc_ref, ranges)
    combine_stats((st0, st1, st2, st3), lse_ref, delta_ref)
    dqt[...] = jnp.zeros_like(dqt)

    def per_step(step, _):
        k = jnp.where(step == 0, 0, REACH + 1 - step)
        acc[...] = jnp.zeros_like(acc)
        visit_step(
            place_ref[1], k, (jnp.where(step == 0, THERE[0], 0), SLAB), ranges,
            (lse_ref, delta_ref, tops, weights, qg_all, kv_all), dqt, acc,
        )

        @pl.when(step == 0)
        def _():
            acc0_ref[...] = acc[...]

        for slot, ref in enumerate((dkv5, dkv34.at[1], dkv34.at[0])):

            @pl.when(step == slot + 1)
            def _():
                write_dkv(ref, acc)

        return 0

    lax.fori_loop(0, HALF + 1, per_step, 0)


def near_kernel(
    place_ref, doc_ref, dqt_in, lse_ref, delta_ref, tops, weights, qg_all, kv_all,
    dqt, across_ref, both_ref, dkv1, dkv2, acc, ranges,
):
    del dqt_in
    step_ranges(place_ref, doc_ref, ranges)

    def per_step(step, _):
        k = 2 - step
        acc[...] = jnp.zeros_like(acc)
        visit_step(
            place_ref[1], k, (0, SLAB), ranges,
            (lse_ref, delta_ref, tops, weights, qg_all, kv_all), dqt, acc,
        )

        @pl.when(k == 2)
        def _():
            write_dkv(dkv2, acc)

        @pl.when(k == 1)
        def _():
            write_dkv(dkv1, acc)

        return 0

    lax.fori_loop(0, 2, per_step, 0)
    write_dq(dqt, 2, across_ref)
    write_dq(dqt, 3, both_ref)


def own_kernel(
    place_ref, doc_ref, dqt_in, lse_ref, delta_ref, tops, weights, qg_all, kv_all, acc0,
    dqt, keep_ref, send_ref, dkv_ref, acc, ranges,
):
    del dqt_in
    step_ranges(place_ref, doc_ref, ranges)
    acc[...] = acc0[...]
    visit_step(
        place_ref[1], jnp.int32(0), HERE, ranges,
        (lse_ref, delta_ref, tops, weights, qg_all, kv_all), dqt, acc,
    )
    write_dkv(dkv_ref, acc)
    write_dq(dqt, 0, keep_ref)
    write_dq(dqt, 1, send_ref)


def merge_kernel(keep, beside, across, both, dkv0, got1, got2, got5, out_ref):
    parts, part = out_ref.shape[:2]
    width = GROUP * HD
    dq = keep[...].astype(F32) + beside[...].astype(F32)
    dq = dq + across[...].astype(F32) + both[...].astype(F32)
    dkv = dkv0[...] + got1[...].astype(F32) + got2[...].astype(F32) + got5[...].astype(F32)
    out_ref[:, :, :width] = dq.astype(BF16).reshape(parts, part, width)
    out_ref[:, :, width:] = dkv.astype(BF16).reshape(parts, part, 2 * HD)


def finish_kernel(got, q_ref, k_ref, v_ref):
    width = GROUP * HD
    for t in range(got.shape[0]):
        q_ref[:, t * width : (t + 1) * width] = got[t, :, :width]
        k_ref[:, t * HD : (t + 1) * HD] = got[t, :, width : width + HD]
        v_ref[:, t * HD : (t + 1) * HD] = got[t, :, width + HD :]


SMEM_SPEC = pl.BlockSpec(memory_space=pltpu.SMEM)
VMEM_SPEC = pl.BlockSpec(memory_space=pltpu.VMEM)


def call(kernel, name, outs, scratch, *args, scalars=2, aliases=None, ranges=True):
    return pl.pallas_call(
        kernel,
        out_shape=tuple(jax.ShapeDtypeStruct(shape, dtype) for shape, dtype in outs),
        in_specs=[SMEM_SPEC] * scalars + [VMEM_SPEC] * (len(args) - scalars),
        out_specs=(VMEM_SPEC,) * len(outs),
        scratch_shapes=[pltpu.VMEM(shape, dtype) for shape, dtype in scratch]
        + [pltpu.SMEM((2 * SLAB,), jnp.int32)] * ranges,
        input_output_aliases=aliases or {},
        compiler_params=pltpu.CompilerParams(vmem_limit_bytes=VMEM_LIMIT),
        cost_estimate=pl.CostEstimate(flops=1, bytes_accessed=1, transcendentals=0),
        name=name,
    )(*args)


QG_ALL = ((SLAB, ROWS, 2 * GROUP * HD), BF16)
KV_ALL = ((REACH + 1, ROWS, 2 * HD), BF16)
STATS = ((3, SLAB * GROUP, ROWS), F32)
TOPS = ((REACH + 1, SLAB * GROUP, ROWS), F32)
WEIGHTS = ((SLAB * (REACH + 1), GROUP, ROWS, ROWS), BF16)
ROW_STATS = ((SLAB * GROUP, ROWS), F32)
DQT = ((SLAB * GROUP, HD, ROWS), F32)
ACC = ((ROWS, 2 * HD), F32)
DKV = ((ROWS, 2 * HD), BF16)
DQ = ((ROWS, GROUP * HD), BF16)


def flip(x, axis):
    return lax.ppermute(x, axis, [(0, 1), (1, 0)])


def shift(x, by, slabs):
    pairs = [(i, i + by) for i in range(slabs) if 0 <= i + by < slabs]
    return lax.ppermute(x, "z", pairs)


def wrapped(x, by, sources, slabs):
    return lax.ppermute(x, "z", [(i, (i + by) % slabs) for i in sources])


def shift_last(x, by, slabs):
    last = SLAB - 1
    pairs = [
        (i * SLAB + last, (i + by) * SLAB + last) for i in range(slabs) if 0 <= i + by < slabs
    ]
    return lax.ppermute(x, ("z", "y", "core"), pairs)


def local(queries, keys, values, grad_out, doc_lengths):
    z = lax.axis_index("z")
    j = lax.axis_index(("y", "core"))
    slabs = lax.axis_size("z")
    place = jnp.stack((z, j)).astype(jnp.int32)

    qg, kv = pl.pallas_call(
        pack_kernel,
        out_shape=(
            jax.ShapeDtypeStruct((ROWS, 2 * GROUP * HD), BF16),
            jax.ShapeDtypeStruct((ROWS, 2 * HD), BF16),
        ),
        in_specs=[pl.BlockSpec(memory_space=pltpu.HBM)] * 4,
        out_specs=(VMEM_SPEC,) * 2,
        scratch_shapes=[pltpu.SemaphoreType.DMA((4,))],
        compiler_params=pltpu.CompilerParams(vmem_limit_bytes=56 * 1024 * 1024),
        cost_estimate=pl.CostEstimate(flops=1, bytes_accessed=1, transcendentals=0),
        name="pack",
    )(queries, grad_out, keys, values)
    across = flip(qg, "y")
    kv1 = shift(kv, 1, slabs)
    kv2 = shift(kv, 2, slabs)
    beside = flip(qg, "core")
    kv5 = shift_last(kv, 5, slabs)
    ahead = [i for i in range(slabs) if i + 4 < slabs]
    kv_by = wrapped(kv, -2, ahead, slabs)

    stats, tops, weights, qg_all, kv_all = call(
        first_stats_kernel, "first_statistics", [STATS, TOPS, WEIGHTS, QG_ALL, KV_ALL], [],
        place, doc_lengths, qg, beside, kv,
    )
    across, kv1, kv2, kv5, kv_by, stats = lax.optimization_barrier(
        (across, kv1, kv2, kv5, kv_by, stats)
    )
    kv3 = shift(kv2, 1, slabs)
    kv4 = wrapped(kv_by, -2, [(i - 2) % slabs for i in ahead], slabs)
    both = flip(across, "core")
    stats, tops, weights, kv_all = call(
        here_stats_kernel, "here_statistics", [STATS, TOPS, WEIGHTS, KV_ALL], [],
        place, doc_lengths, stats, tops, weights, kv_all, qg_all, kv1, kv2,
        aliases={2: 0, 3: 1, 4: 2, 5: 3},
    )
    stats, tops, weights, qg_all = call(
        there_stats_kernel, "there_statistics", [STATS, TOPS, WEIGHTS, QG_ALL], [],
        place, doc_lengths, stats, tops, weights, qg_all, kv_all, across, both,
        aliases={2: 0, 3: 1, 4: 2, 5: 3},
    )
    stats, tops, weights, kv_all = call(
        far_stats_kernel, "far_statistics", [STATS, TOPS, WEIGHTS, KV_ALL], [],
        place, doc_lengths, stats, tops, weights, kv_all, qg_all, kv3, kv4, kv5,
        aliases={2: 0, 3: 1, 4: 2, 5: 3},
    )
    stats_y = flip(stats, "y")
    stats_c = flip(stats, "core")
    stats_yc = flip(stats_y, "core")

    data = (tops, weights, qg_all, kv_all)
    dqt, dkv34, dkv5, acc0, lse, delta = call(
        far_kernel, "far_gradients",
        [DQT, ((2,) + DKV[0], BF16), DKV, ACC, ROW_STATS, ROW_STATS], [ACC],
        place, doc_lengths, stats, stats_c, stats_y, stats_yc, *data,
    )
    got_far = shift(dkv34, -2, slabs)
    got5 = shift_last(dkv5, -5, slabs)
    dqt, dq_across, dq_both, dkv1, dkv2 = call(
        near_kernel, "near_gradients", [DQT, DQ, DQ, ACC, ACC], [ACC],
        place, doc_lengths, dqt, lse, delta, *data, aliases={2: 0},
    )
    dq_across = flip(dq_across, "y")
    dq_both = lax.ppermute(dq_both, ("y", "core"), [(i, i ^ 3) for i in range(SLAB)])
    dkv1 = (dkv1 + got_far[0].astype(F32)).astype(BF16)
    dkv2 = (dkv2 + got_far[1].astype(F32)).astype(BF16)
    got2 = shift(dkv2, -2, slabs)
    got1 = shift(dkv1, -1, slabs)
    _, dq_keep, dq_send, dkv0 = call(
        own_kernel, "own_gradients", [DQT, DQ, DQ, ACC], [ACC],
        place, doc_lengths, dqt, lse, delta, *data, acc0, aliases={2: 0},
    )
    dq_beside = flip(dq_send, "core")
    got1, got2, got5, dq_across, dq_both, dq_beside = lax.optimization_barrier(
        (got1, got2, got5, dq_across, dq_both, dq_beside)
    )

    tp = lax.axis_size("tp")
    part = ROWS // tp
    width = GROUP * HD
    whole, = call(
        merge_kernel, "merge", [((tp, part, width + 2 * HD), BF16)], [],
        dq_keep, dq_beside, dq_across, dq_both, dkv0, got1, got2, got5, scalars=0, ranges=False,
    )
    got = lax.all_to_all(whole, "tp", split_axis=0, concat_axis=0, tiled=True)
    return call(
        finish_kernel, "finish",
        [((part, tp * width), BF16), ((part, tp * HD), BF16), ((part, tp * HD), BF16)], [],
        got, scalars=0, ranges=False,
    )


def solution(mesh):
    tp = mesh.shape["tp"]
    inner = Mesh(mesh.devices.reshape(-1, 2, 2, tp), ("z", "y", "core", "tp"))
    tokens = ("z", "y", "core")
    in_specs = (P(tokens, "tp"),) * 4 + (P(),)
    out_specs = (P(tokens + ("tp",), None),) * 3
    return jax.shard_map(local, mesh=inner, in_specs=in_specs, out_specs=out_specs, check_vma=False)
```

```python
import math

import jax
import jax.numpy as jnp
from jax import lax
from jax.experimental import pallas as pl
from jax.experimental.pallas import tpu as pltpu
from jax.sharding import Mesh, PartitionSpec as P

HD = 128
GROUP = 4
ROWS = 256
SLAB = 4
REACH = 5
HALF = 3
HERE = (0, 2)
THERE = (2, 4)
DOC_COUNT = 17
SCALE = HD ** -0.5
SCALE2 = SCALE * math.log2(math.e)
MASKED = -1e30
EMPTY = -1e29
VMEM_LIMIT = 16 * 1024 * 1024
NT = (((1,), (1,)), ((), ()))
NN = (((1,), (0,)), ((), ()))
F32 = jnp.float32
BF16 = jnp.bfloat16


def dot_nt(a, b):
    return lax.dot_general(a, b, NT, preferred_element_type=F32)


def dot_nn(a, b):
    return lax.dot_general(a, b, NN, preferred_element_type=F32)


def start_of(doc_ref, positions):
    end = jnp.int32(0)
    starts = jnp.zeros_like(positions)
    for doc in range(DOC_COUNT):
        length = doc_ref[doc]
        end = end + length
        starts = starts + jnp.where(end <= positions, length, 0)
    return starts


def step_ranges(place_ref, doc_ref, steps_ref):
    z, j = place_ref[0], place_ref[1]
    for rel in range(SLAB):
        qb = j ^ rel
        first = start_of(doc_ref, (SLAB * z + qb) * ROWS) // ROWS
        steps_ref[2 * rel] = jnp.where(j <= qb, 0, 1)
        steps_ref[2 * rel + 1] = z - jnp.maximum((first - j + SLAB - 1) >> 2, 0)


def pack_kernel(q_ref, g_ref, k_ref, v_ref, qg_ref, kv_ref, sems):
    wide, thin = GROUP * HD, HD
    copies = [
        pltpu.make_async_copy(k_ref, kv_ref.at[:, :thin], sems.at[0]),
        pltpu.make_async_copy(v_ref, kv_ref.at[:, thin:], sems.at[1]),
        pltpu.make_async_copy(q_ref, qg_ref.at[:, :wide], sems.at[2]),
        pltpu.make_async_copy(g_ref, qg_ref.at[:, wide:], sems.at[3]),
    ]
    for copy in copies:
        copy.start()
    for copy in copies:
        copy.wait()


def stats_steps(place_ref, doc_ref, rels, steps, fresh, qg, kv, tops, weights, out_ref, ranges):
    z, j = place_ref[0], place_ref[1]
    step_ranges(place_ref, doc_ref, ranges)

    def per_block(rel, _):
        qb = j ^ rel
        positions = (SLAB * z + qb) * ROWS + lax.broadcasted_iota(jnp.int32, (1, ROWS), 1)
        starts = start_of(doc_ref, positions)

        def per_step(k, carry):
            key_pos = lax.broadcasted_iota(jnp.int32, (ROWS, ROWS), 0)
            offset = (SLAB * (z - k) + j) * ROWS
            mask = (key_pos >= starts - offset) & (key_pos <= positions - offset)
            keys = kv[k, :, :HD]
            values = kv[k, :, HD:]

            def products(h):
                q = qg[rel, :, h * HD : (h + 1) * HD]
                g = qg[rel, :, (GROUP + h) * HD : (GROUP + h + 1) * HD]
                return dot_nt(keys, q), dot_nt(values, g)

            new = []
            ahead = products(0)
            for h in range(GROUP):
                s, dp = ahead
                if h + 1 < GROUP:
                    ahead = products(h + 1)
                top, total, dot = carry[3 * h : 3 * h + 3]
                s = jnp.where(mask, s * SCALE2, MASKED)
                new_top = jnp.maximum(top, jnp.max(s, axis=0, keepdims=True))
                p = jnp.exp2(s - new_top)
                weights[rel * (REACH + 1) + k, h] = p.astype(BF16)
                tops[k, pl.ds(rel * GROUP + h, 1), :] = new_top
                factor = jnp.exp2(top - new_top)
                new += [
                    new_top,
                    total * factor + jnp.sum(p, axis=0, keepdims=True),
                    dot * factor + jnp.sum(p * dp, axis=0, keepdims=True),
                ]
            return tuple(new)

        if fresh:
            zero = jnp.zeros((1, ROWS), F32)
            init = (jnp.full((1, ROWS), EMPTY, F32), zero, zero) * GROUP
        else:
            init = tuple(
                out_ref[part, pl.ds(qb * GROUP + h, 1), :]
                for h in range(GROUP)
                for part in range(3)
            )
        first = jnp.maximum(ranges[2 * rel], steps[0])
        end = jnp.minimum(ranges[2 * rel + 1] + 1, steps[1])
        done = lax.fori_loop(first, end, per_step, init)
        for h in range(GROUP):
            for part in range(3):
                out_ref[part, pl.ds(qb * GROUP + h, 1), :] = done[3 * h + part]
        return 0

    lax.fori_loop(rels[0], rels[1], per_block, 0)


def first_stats_kernel(
    place_ref, doc_ref, qg0, qg1, kv0, out_ref, tops, weights, qg_all, kv_all, ranges
):
    qg_all[0] = qg0[...]
    qg_all[1] = qg1[...]
    kv_all[0] = kv0[...]
    stats_steps(
        place_ref, doc_ref, HERE, (0, 1), True, qg_all, kv_all, tops, weights, out_ref, ranges
    )


def here_stats_kernel(
    place_ref, doc_ref, in0, in1, in2, in3, qg_all, kv1, kv2, out_ref, tops, weights, kv_all, ranges
):
    del in0, in1, in2, in3
    kv_all[1] = kv1[...]
    kv_all[2] = kv2[...]
    stats_steps(
        place_ref, doc_ref, HERE, (1, HALF), False, qg_all, kv_all, tops, weights, out_ref, ranges
    )


def there_stats_kernel(
    place_ref, doc_ref, in0, in1, in2, in3, kv_all, qg2, qg3, out_ref, tops, weights, qg_all, ranges
):
    del in0, in1, in2, in3
    qg_all[2] = qg2[...]
    qg_all[3] = qg3[...]
    stats_steps(
        place_ref, doc_ref, THERE, (0, HALF), True, qg_all, kv_all, tops, weights, out_ref, ranges
    )


def far_stats_kernel(
    place_ref, doc_ref, in0, in1, in2, in3, qg_all, kv3, kv4, kv5,
    out_ref, tops, weights, kv_all, ranges,
):
    del in0, in1, in2, in3
    for slot, ref in enumerate((kv3, kv4, kv5)):
        kv_all[HALF + slot] = ref[...]
    stats_steps(
        place_ref, doc_ref, (0, SLAB), (HALF, REACH + 1), False,
        qg_all, kv_all, tops, weights, out_ref, ranges,
    )


def combine_stats(st_refs, lse_buf, delta_buf):
    stats = [ref[...] for ref in st_refs]
    top = jnp.maximum(
        jnp.maximum(stats[0][0], stats[1][0]), jnp.maximum(stats[2][0], stats[3][0])
    )
    total = jnp.zeros_like(top)
    dot = jnp.zeros_like(top)
    for st in stats:
        factor = jnp.exp2(st[0] - top)
        total = total + st[1] * factor
        dot = dot + st[2] * factor
    lse_buf[...] = top + jnp.log2(total)
    delta_buf[...] = dot / total


def visit_step(j, k, rels, ranges, data, dqt, acc):
    lse_buf, delta_buf, tops, weights, qg_all, kv_all = data
    keys_t = kv_all[k, :, :HD].astype(F32).T.astype(BF16)

    def per_block(rel, _):
        qb = j ^ rel

        @pl.when((k >= ranges[2 * rel]) & (k <= ranges[2 * rel + 1]))
        def _():
            values = kv_all[k, :, HD:]

            def grad_of(h):
                return qg_all[rel, :, (GROUP + h) * HD : (GROUP + h + 1) * HD]

            dk = dv = None
            ahead = dot_nt(values, grad_of(0))
            for h in range(GROUP):
                dp = ahead
                if h + 1 < GROUP:
                    ahead = dot_nt(values, grad_of(h + 1))
                q = qg_all[rel, :, h * HD : (h + 1) * HD]
                lse = lse_buf[pl.ds(qb * GROUP + h, 1), :]
                delta = delta_buf[pl.ds(qb * GROUP + h, 1), :]
                factor = jnp.exp2(tops[k, pl.ds(rel * GROUP + h, 1), :] - lse)
                p = weights[rel * (REACH + 1) + k, h].astype(F32) * factor
                ds = p * (dp - delta)
                pb = p.astype(BF16)
                dsb = ds.astype(BF16)
                dv_add, dk_add = dot_nn(pb, grad_of(h)), dot_nn(dsb, q)
                dv = dv_add if dv is None else dv + dv_add
                dk = dk_add if dk is None else dk + dk_add
                dqt[rel * GROUP + h] += dot_nn(keys_t, dsb)
            acc[:, :HD] += dk
            acc[:, HD:] += dv

        return 0

    lax.fori_loop(rels[0], rels[1], per_block, 0)


def write_dq(dqt, slot, out_ref):
    for h in range(GROUP):
        dq = dqt[slot * GROUP + h].T * SCALE
        out_ref[:, h * HD : (h + 1) * HD] = dq.astype(BF16)


def write_dkv(out_ref, acc):
    out_ref[:, :HD] = (acc[:, :HD] * SCALE).astype(out_ref.dtype)
    out_ref[:, HD:] = acc[:, HD:].astype(out_ref.dtype)


def far_kernel(
    place_ref, doc_ref, st0, st1, st2, st3, tops, weights, qg_all, kv_all,
    dqt, dkv34, dkv5, acc0_ref, lse_ref, delta_ref, acc, ranges,
):
    step_ranges(place_ref, doc_ref, ranges)
    combine_stats((st0, st1, st2, st3), lse_ref, delta_ref)
    dqt[...] = jnp.zeros_like(dqt)

    def per_step(step, _):
        k = jnp.where(step == 0, 0, REACH + 1 - step)
        acc[...] = jnp.zeros_like(acc)
        visit_step(
            place_ref[1], k, (jnp.where(step == 0, THERE[0], 0), SLAB), ranges,
            (lse_ref, delta_ref, tops, weights, qg_all, kv_all), dqt, acc,
        )

        @pl.when(step == 0)
        def _():
            acc0_ref[...] = acc[...]

        for slot, ref in enumerate((dkv5, dkv34.at[1], dkv34.at[0])):

            @pl.when(step == slot + 1)
            def _():
                write_dkv(ref, acc)

        return 0

    lax.fori_loop(0, HALF + 1, per_step, 0)


def there_kernel(
    place_ref, doc_ref, dqt_in, lse_ref, delta_ref, tops, weights, qg_all, kv_all,
    dqt, keep_ref, send_ref, acc_ref, acc, ranges,
):
    del dqt_in
    step_ranges(place_ref, doc_ref, ranges)

    def per_step(step, _):
        k = 2 - step
        acc[...] = jnp.zeros_like(acc)
        visit_step(
            place_ref[1], k, THERE, ranges,
            (lse_ref, delta_ref, tops, weights, qg_all, kv_all), dqt, acc,
        )
        acc_ref[k - 1] = acc[...]
        return 0

    lax.fori_loop(0, 2, per_step, 0)
    write_dq(dqt, 2, keep_ref)
    write_dq(dqt, 3, send_ref)


def here_kernel(
    place_ref, doc_ref, dqt_in, lse_ref, delta_ref, tops, weights, qg_all, kv_all, acc0, acc_near,
    dqt, beside_ref, dkv1, dkv2, acc0_out, acc, ranges,
):
    del dqt_in
    step_ranges(place_ref, doc_ref, ranges)

    def per_step(step, _):
        k = 2 - step

        @pl.when(k > 0)
        def _():
            acc[...] = acc_near[jnp.maximum(k - 1, 0)]

        @pl.when(k == 0)
        def _():
            acc[...] = acc0[...]

        visit_step(
            place_ref[1], k, (jnp.where(k == 0, 1, 0), HERE[1]), ranges,
            (lse_ref, delta_ref, tops, weights, qg_all, kv_all), dqt, acc,
        )

        @pl.when(k == 2)
        def _():
            write_dkv(dkv2, acc)

        @pl.when(k == 1)
        def _():
            write_dkv(dkv1, acc)

        return 0

    lax.fori_loop(0, 3, per_step, 0)
    acc0_out[...] = acc[...]
    write_dq(dqt, 1, beside_ref)


def own_kernel(
    place_ref, doc_ref, dqt_in, lse_ref, delta_ref, tops, weights, qg_all, kv_all, acc0,
    dqt, dq_ref, dkv_ref, acc, ranges,
):
    del dqt_in
    step_ranges(place_ref, doc_ref, ranges)
    acc[...] = acc0[...]
    visit_step(
        place_ref[1], jnp.int32(0), (0, 1), ranges,
        (lse_ref, delta_ref, tops, weights, qg_all, kv_all), dqt, acc,
    )
    write_dkv(dkv_ref, acc)
    write_dq(dqt, 0, dq_ref)


def pair_kernel(keep, got, out_ref):
    out_ref[...] = (keep[...].astype(F32) + got[...].astype(F32)).astype(BF16)


def merge_kernel(keep, beside, across, dkv0, got1, got2, got5, out_ref):
    parts, part = out_ref.shape[:2]
    width = GROUP * HD
    dkv = dkv0[...] + got1[...].astype(F32) + got2[...].astype(F32) + got5[...].astype(F32)
    dq = keep[...].astype(F32) + beside[...].astype(F32) + across[...].astype(F32)
    out_ref[:, :, :width] = dq.astype(BF16).reshape(parts, part, width)
    out_ref[:, :, width:] = dkv.astype(BF16).reshape(parts, part, 2 * HD)


def finish_kernel(got, q_ref, k_ref, v_ref):
    width = GROUP * HD
    for t in range(got.shape[0]):
        q_ref[:, t * width : (t + 1) * width] = got[t, :, :width]
        k_ref[:, t * HD : (t + 1) * HD] = got[t, :, width : width + HD]
        v_ref[:, t * HD : (t + 1) * HD] = got[t, :, width + HD :]


SMEM_SPEC = pl.BlockSpec(memory_space=pltpu.SMEM)
VMEM_SPEC = pl.BlockSpec(memory_space=pltpu.VMEM)


def call(kernel, name, outs, scratch, *args, scalars=2, aliases=None, ranges=True):
    return pl.pallas_call(
        kernel,
        out_shape=tuple(jax.ShapeDtypeStruct(shape, dtype) for shape, dtype in outs),
        in_specs=[SMEM_SPEC] * scalars + [VMEM_SPEC] * (len(args) - scalars),
        out_specs=(VMEM_SPEC,) * len(outs),
        scratch_shapes=[pltpu.VMEM(shape, dtype) for shape, dtype in scratch]
        + [pltpu.SMEM((2 * SLAB,), jnp.int32)] * ranges,
        input_output_aliases=aliases or {},
        compiler_params=pltpu.CompilerParams(vmem_limit_bytes=VMEM_LIMIT),
        cost_estimate=pl.CostEstimate(flops=1, bytes_accessed=1, transcendentals=0),
        name=name,
    )(*args)


QG_ALL = ((SLAB, ROWS, 2 * GROUP * HD), BF16)
KV_ALL = ((REACH + 1, ROWS, 2 * HD), BF16)
STATS = ((3, SLAB * GROUP, ROWS), F32)
TOPS = ((REACH + 1, SLAB * GROUP, ROWS), F32)
WEIGHTS = ((SLAB * (REACH + 1), GROUP, ROWS, ROWS), BF16)
ROW_STATS = ((SLAB * GROUP, ROWS), F32)
DQT = ((SLAB * GROUP, HD, ROWS), F32)
ACC = ((ROWS, 2 * HD), F32)
DKV = ((ROWS, 2 * HD), BF16)
DQ = ((ROWS, GROUP * HD), BF16)


def flip(x, axis):
    return lax.ppermute(x, axis, [(0, 1), (1, 0)])


def shift(x, by, slabs):
    pairs = [(i, i + by) for i in range(slabs) if 0 <= i + by < slabs]
    return lax.ppermute(x, "z", pairs)


def wrapped(x, by, sources, slabs):
    return lax.ppermute(x, "z", [(i, (i + by) % slabs) for i in sources])


def shift_last(x, by, slabs):
    last = SLAB - 1
    pairs = [
        (i * SLAB + last, (i + by) * SLAB + last) for i in range(slabs) if 0 <= i + by < slabs
    ]
    return lax.ppermute(x, ("z", "y", "core"), pairs)


def local(queries, keys, values, grad_out, doc_lengths):
    z = lax.axis_index("z")
    j = lax.axis_index(("y", "core"))
    slabs = lax.axis_size("z")
    place = jnp.stack((z, j)).astype(jnp.int32)

    qg, kv = pl.pallas_call(
        pack_kernel,
        out_shape=(
            jax.ShapeDtypeStruct((ROWS, 2 * GROUP * HD), BF16),
            jax.ShapeDtypeStruct((ROWS, 2 * HD), BF16),
        ),
        in_specs=[pl.BlockSpec(memory_space=pltpu.HBM)] * 4,
        out_specs=(VMEM_SPEC,) * 2,
        scratch_shapes=[pltpu.SemaphoreType.DMA((4,))],
        compiler_params=pltpu.CompilerParams(vmem_limit_bytes=56 * 1024 * 1024),
        cost_estimate=pl.CostEstimate(flops=1, bytes_accessed=1, transcendentals=0),
        name="pack",
    )(queries, grad_out, keys, values)
    across = flip(qg, "y")
    kv1 = shift(kv, 1, slabs)
    kv2 = shift(kv, 2, slabs)
    beside = flip(qg, "core")
    kv5 = shift_last(kv, 5, slabs)
    ahead = [i for i in range(slabs) if i + 4 < slabs]
    kv_by = wrapped(kv, -2, ahead, slabs)

    stats, tops, weights, qg_all, kv_all = call(
        first_stats_kernel, "first_statistics", [STATS, TOPS, WEIGHTS, QG_ALL, KV_ALL], [],
        place, doc_lengths, qg, beside, kv,
    )
    across, kv1, kv2, kv5, kv_by, stats = lax.optimization_barrier(
        (across, kv1, kv2, kv5, kv_by, stats)
    )
    kv3 = shift(kv2, 1, slabs)
    kv4 = wrapped(kv_by, -2, [(i - 2) % slabs for i in ahead], slabs)
    both = flip(across, "core")
    stats, tops, weights, kv_all = call(
        here_stats_kernel, "here_statistics", [STATS, TOPS, WEIGHTS, KV_ALL], [],
        place, doc_lengths, stats, tops, weights, kv_all, qg_all, kv1, kv2,
        aliases={2: 0, 3: 1, 4: 2, 5: 3},
    )
    stats, tops, weights, qg_all = call(
        there_stats_kernel, "there_statistics", [STATS, TOPS, WEIGHTS, QG_ALL], [],
        place, doc_lengths, stats, tops, weights, qg_all, kv_all, across, both,
        aliases={2: 0, 3: 1, 4: 2, 5: 3},
    )
    stats, tops, weights, kv_all = call(
        far_stats_kernel, "far_statistics", [STATS, TOPS, WEIGHTS, KV_ALL], [],
        place, doc_lengths, stats, tops, weights, kv_all, qg_all, kv3, kv4, kv5,
        aliases={2: 0, 3: 1, 4: 2, 5: 3},
    )
    stats_y = flip(stats, "y")
    stats_c = flip(stats, "core")
    stats_yc = flip(stats_y, "core")

    data = (tops, weights, qg_all, kv_all)
    dqt, dkv34, dkv5, acc0, lse, delta = call(
        far_kernel, "far_gradients",
        [DQT, ((2,) + DKV[0], BF16), DKV, ACC, ROW_STATS, ROW_STATS], [ACC],
        place, doc_lengths, stats, stats_c, stats_y, stats_yc, *data,
    )
    got_far = shift(dkv34, -2, slabs)
    got5 = shift_last(dkv5, -5, slabs)
    dqt, there_keep, there_send, acc_near = call(
        there_kernel, "there_gradients", [DQT, DQ, DQ, ((2,) + ACC[0], F32)], [ACC],
        place, doc_lengths, dqt, lse, delta, *data, aliases={2: 0},
    )
    there_got = flip(there_send, "core")
    dqt, dq_beside, dkv1, dkv2, acc0 = call(
        here_kernel, "here_gradients", [DQT, DQ, ACC, ACC, ACC], [ACC],
        place, doc_lengths, dqt, lse, delta, *data, acc0, acc_near, aliases={2: 0},
    )
    dkv1 = (dkv1 + got_far[0].astype(F32)).astype(BF16)
    dkv2 = (dkv2 + got_far[1].astype(F32)).astype(BF16)
    there_got, dkv1, dkv2 = lax.optimization_barrier((there_got, dkv1, dkv2))
    dq_pair, = call(
        pair_kernel, "pair", [DQ], [], there_keep, there_got, scalars=0, ranges=False
    )
    dq_across = flip(dq_pair, "y")
    dq_beside = flip(dq_beside, "core")
    got2 = shift(dkv2, -2, slabs)
    got1 = shift(dkv1, -1, slabs)
    _, dq_keep, dkv0 = call(
        own_kernel, "own_gradients", [DQT, DQ, ACC], [ACC],
        place, doc_lengths, dqt, lse, delta, *data, acc0, aliases={2: 0},
    )

    tp = lax.axis_size("tp")
    part = ROWS // tp
    width = GROUP * HD
    whole, = call(
        merge_kernel, "merge", [((tp, part, width + 2 * HD), BF16)], [],
        dq_keep, dq_beside, dq_across, dkv0, got1, got2, got5, scalars=0, ranges=False,
    )
    got = lax.all_to_all(whole, "tp", split_axis=0, concat_axis=0, tiled=True)
    return call(
        finish_kernel, "finish",
        [((part, tp * width), BF16), ((part, tp * HD), BF16), ((part, tp * HD), BF16)], [],
        got, scalars=0, ranges=False,
    )


def solution(mesh):
    tp = mesh.shape["tp"]
    inner = Mesh(mesh.devices.reshape(-1, 2, 2, tp), ("z", "y", "core", "tp"))
    tokens = ("z", "y", "core")
    in_specs = (P(tokens, "tp"),) * 4 + (P(),)
    out_specs = (P(tokens + ("tp",), None),) * 3
    return jax.shard_map(local, mesh=inner, in_specs=in_specs, out_specs=out_specs, check_vma=False)
```

```python
import math

import jax
import jax.numpy as jnp
from jax import lax
from jax.experimental import pallas as pl
from jax.experimental.pallas import tpu as pltpu
from jax.sharding import Mesh, PartitionSpec as P

HD = 128
GROUP = 4
ROWS = 256
SLAB = 4
REACH = 5
HALF = 3
HERE = (0, 2)
THERE = (2, 4)
DOC_COUNT = 17
SCALE = HD ** -0.5
SCALE2 = SCALE * math.log2(math.e)
MASKED = -1e30
EMPTY = -1e29
VMEM_LIMIT = 16 * 1024 * 1024
NT = (((1,), (1,)), ((), ()))
NN = (((1,), (0,)), ((), ()))
F32 = jnp.float32
BF16 = jnp.bfloat16


def dot_nt(a, b):
    return lax.dot_general(a, b, NT, preferred_element_type=F32)


def dot_nn(a, b):
    return lax.dot_general(a, b, NN, preferred_element_type=F32)


def start_of(doc_ref, positions):
    end = jnp.int32(0)
    starts = jnp.zeros_like(positions)
    for doc in range(DOC_COUNT):
        length = doc_ref[doc]
        end = end + length
        starts = starts + jnp.where(end <= positions, length, 0)
    return starts


def find_starts(place_ref, doc_ref, starts_ref, ranges_ref):
    z, j = place_ref[0], place_ref[1]
    for rel in range(SLAB):
        qb = j ^ rel
        first = start_of(doc_ref, (SLAB * z + qb) * ROWS) // ROWS
        ranges_ref[2 * rel] = jnp.where(j <= qb, 0, 1)
        ranges_ref[2 * rel + 1] = z - jnp.maximum((first - j + SLAB - 1) >> 2, 0)
        starts_ref[rel : rel + 1, :] = start_of(doc_ref, query_positions(z, qb))


def query_positions(z, qb):
    return (SLAB * z + qb) * ROWS + lax.broadcasted_iota(jnp.int32, (1, ROWS), 1)


def pack_kernel(q_ref, g_ref, k_ref, v_ref, qg_ref, kv_ref, sems):
    wide, thin = GROUP * HD, HD
    copies = [
        pltpu.make_async_copy(k_ref, kv_ref.at[:, :thin], sems.at[0]),
        pltpu.make_async_copy(v_ref, kv_ref.at[:, thin:], sems.at[1]),
        pltpu.make_async_copy(q_ref, qg_ref.at[:, :wide], sems.at[2]),
        pltpu.make_async_copy(g_ref, qg_ref.at[:, wide:], sems.at[3]),
    ]
    for copy in copies:
        copy.start()
    for copy in copies:
        copy.wait()


def stats_steps(place_ref, where, rels, steps, fresh, qg, kv, tops, weights, out_ref):
    z, j = place_ref[0], place_ref[1]
    ranges, starts_ref = where

    def per_block(rel, _):
        qb = j ^ rel
        positions = query_positions(z, qb)
        starts = starts_ref[pl.ds(rel, 1), :]

        def per_step(k, carry):
            key_pos = lax.broadcasted_iota(jnp.int32, (ROWS, ROWS), 0)
            offset = (SLAB * (z - k) + j) * ROWS
            mask = (key_pos >= starts - offset) & (key_pos <= positions - offset)
            keys = kv[k, :, :HD]
            values = kv[k, :, HD:]

            def products(h):
                q = qg[rel, :, h * HD : (h + 1) * HD]
                g = qg[rel, :, (GROUP + h) * HD : (GROUP + h + 1) * HD]
                return dot_nt(keys, q), dot_nt(values, g)

            new = []
            ahead = products(0)
            for h in range(GROUP):
                s, dp = ahead
                if h + 1 < GROUP:
                    ahead = products(h + 1)
                top, total, dot = carry[3 * h : 3 * h + 3]
                s = jnp.where(mask, s * SCALE2, MASKED)
                new_top = jnp.maximum(top, jnp.max(s, axis=0, keepdims=True))
                p = jnp.exp2(s - new_top)
                weights[rel * (REACH + 1) + k, h] = p.astype(BF16)
                tops[k, pl.ds(rel * GROUP + h, 1), :] = new_top
                factor = jnp.exp2(top - new_top)
                new += [
                    new_top,
                    total * factor + jnp.sum(p, axis=0, keepdims=True),
                    dot * factor + jnp.sum(p * dp, axis=0, keepdims=True),
                ]
            return tuple(new)

        if fresh:
            zero = jnp.zeros((1, ROWS), F32)
            init = (jnp.full((1, ROWS), EMPTY, F32), zero, zero) * GROUP
        else:
            init = tuple(
                out_ref[part, pl.ds(qb * GROUP + h, 1), :]
                for h in range(GROUP)
                for part in range(3)
            )
        first = jnp.maximum(ranges[2 * rel], steps[0])
        end = jnp.minimum(ranges[2 * rel + 1] + 1, steps[1])
        done = lax.fori_loop(first, end, per_step, init)
        for h in range(GROUP):
            for part in range(3):
                out_ref[part, pl.ds(qb * GROUP + h, 1), :] = done[3 * h + part]
        return 0

    lax.fori_loop(rels[0], rels[1], per_block, 0)


def first_stats_kernel(
    place_ref, doc_ref, qg0, qg1, kv0, ranges, starts, out_ref, tops, weights, qg_all, kv_all
):
    find_starts(place_ref, doc_ref, starts, ranges)
    qg_all[0] = qg0[...]
    qg_all[1] = qg1[...]
    kv_all[0] = kv0[...]
    stats_steps(
        place_ref, (ranges, starts), HERE, (0, 1), True, qg_all, kv_all, tops, weights, out_ref
    )


def here_stats_kernel(
    place_ref, ranges, in0, in1, in2, in3, starts, qg_all, kv1, kv2, out_ref, tops, weights, kv_all
):
    del in0, in1, in2, in3
    kv_all[1] = kv1[...]
    kv_all[2] = kv2[...]
    stats_steps(
        place_ref, (ranges, starts), HERE, (1, HALF), False,
        qg_all, kv_all, tops, weights, out_ref,
    )


def there_stats_kernel(
    place_ref, ranges, in0, in1, in2, in3, starts, kv_all, qg2, qg3, out_ref, tops, weights, qg_all
):
    del in0, in1, in2, in3
    qg_all[2] = qg2[...]
    qg_all[3] = qg3[...]
    stats_steps(
        place_ref, (ranges, starts), THERE, (0, HALF), True,
        qg_all, kv_all, tops, weights, out_ref,
    )


def far_stats_kernel(
    place_ref, ranges, in0, in1, in2, in3, starts, qg_all, kv3, kv4, kv5,
    out_ref, tops, weights, kv_all,
):
    del in0, in1, in2, in3
    for slot, ref in enumerate((kv3, kv4, kv5)):
        kv_all[HALF + slot] = ref[...]
    stats_steps(
        place_ref, (ranges, starts), (0, SLAB), (HALF, REACH + 1), False,
        qg_all, kv_all, tops, weights, out_ref,
    )


def combine_stats(st_refs, lse_buf, delta_buf):
    stats = [ref[...] for ref in st_refs]
    top = jnp.maximum(
        jnp.maximum(stats[0][0], stats[1][0]), jnp.maximum(stats[2][0], stats[3][0])
    )
    total = jnp.zeros_like(top)
    dot = jnp.zeros_like(top)
    for st in stats:
        factor = jnp.exp2(st[0] - top)
        total = total + st[1] * factor
        dot = dot + st[2] * factor
    lse_buf[...] = top + jnp.log2(total)
    delta_buf[...] = dot / total


def visit_step(j, k, rels, ranges, data, dqt, acc):
    lse_buf, delta_buf, tops, weights, qg_all, kv_all = data
    keys_t = kv_all[k, :, :HD].T

    def per_block(rel, _):
        qb = j ^ rel

        @pl.when((k >= ranges[2 * rel]) & (k <= ranges[2 * rel + 1]))
        def _():
            values = kv_all[k, :, HD:]

            def grad_of(h):
                return qg_all[rel, :, (GROUP + h) * HD : (GROUP + h + 1) * HD]

            dk = dv = None
            ahead = dot_nt(values, grad_of(0))
            for h in range(GROUP):
                dp = ahead
                if h + 1 < GROUP:
                    ahead = dot_nt(values, grad_of(h + 1))
                q = qg_all[rel, :, h * HD : (h + 1) * HD]
                lse = lse_buf[pl.ds(qb * GROUP + h, 1), :]
                delta = delta_buf[pl.ds(qb * GROUP + h, 1), :]
                factor = jnp.exp2(tops[k, pl.ds(rel * GROUP + h, 1), :] - lse)
                p = weights[rel * (REACH + 1) + k, h].astype(F32) * factor
                ds = p * (dp - delta)
                pb = p.astype(BF16)
                dsb = ds.astype(BF16)
                dv_add, dk_add = dot_nn(pb, grad_of(h)), dot_nn(dsb, q)
                dv = dv_add if dv is None else dv + dv_add
                dk = dk_add if dk is None else dk + dk_add
                dqt[rel * GROUP + h] += dot_nn(keys_t, dsb)
            acc[:, :HD] += dk
            acc[:, HD:] += dv

        return 0

    lax.fori_loop(rels[0], rels[1], per_block, 0)


def write_dq(dqt, slot, out_ref):
    for h in range(GROUP):
        dq = (dqt[slot * GROUP + h] * SCALE).astype(BF16)
        out_ref[:, h * HD : (h + 1) * HD] = dq.T


def write_dkv(out_ref, acc):
    out_ref[:, :HD] = (acc[:, :HD] * SCALE).astype(out_ref.dtype)
    out_ref[:, HD:] = acc[:, HD:].astype(out_ref.dtype)


def far_kernel(
    place_ref, ranges, st0, st1, st2, st3, tops, weights, qg_all, kv_all,
    dqt, dkv3, dkv4, dkv5, acc0_ref, lse_ref, delta_ref, acc,
):
    combine_stats((st0, st1, st2, st3), lse_ref, delta_ref)
    dqt[...] = jnp.zeros_like(dqt)

    def per_step(step, _):
        k = jnp.where(step == 0, 0, REACH + 1 - step)
        acc[...] = jnp.zeros_like(acc)
        visit_step(
            place_ref[1], k, (jnp.where(step == 0, THERE[0], 0), SLAB), ranges,
            (lse_ref, delta_ref, tops, weights, qg_all, kv_all), dqt, acc,
        )

        @pl.when(step == 0)
        def _():
            acc0_ref[...] = acc[...]

        for slot, ref in enumerate((dkv5, dkv4, dkv3)):

            @pl.when(step == slot + 1)
            def _():
                write_dkv(ref, acc)

        return 0

    lax.fori_loop(0, HALF + 1, per_step, 0)


def there_kernel(
    place_ref, ranges, dqt_in, lse_ref, delta_ref, tops, weights, qg_all, kv_all,
    dqt, keep_ref, send_ref, acc_ref, acc,
):
    del dqt_in

    def per_step(step, _):
        k = 2 - step
        acc[...] = jnp.zeros_like(acc)
        visit_step(
            place_ref[1], k, THERE, ranges,
            (lse_ref, delta_ref, tops, weights, qg_all, kv_all), dqt, acc,
        )
        acc_ref[k - 1] = acc[...]
        return 0

    lax.fori_loop(0, 2, per_step, 0)
    write_dq(dqt, 2, keep_ref)
    write_dq(dqt, 3, send_ref)


def here_kernel(
    place_ref, ranges, dqt_in, lse_ref, delta_ref, tops, weights, qg_all, kv_all, acc0, acc_near,
    dqt, beside_ref, dkv1, dkv2, acc0_out, acc,
):
    del dqt_in

    def per_step(step, _):
        k = 2 - step

        @pl.when(k > 0)
        def _():
            acc[...] = acc_near[jnp.maximum(k - 1, 0)]

        @pl.when(k == 0)
        def _():
            acc[...] = acc0[...]

        visit_step(
            place_ref[1], k, (jnp.where(k == 0, 1, 0), HERE[1]), ranges,
            (lse_ref, delta_ref, tops, weights, qg_all, kv_all), dqt, acc,
        )

        @pl.when(k == 2)
        def _():
            write_dkv(dkv2, acc)

        @pl.when(k == 1)
        def _():
            write_dkv(dkv1, acc)

        return 0

    lax.fori_loop(0, 3, per_step, 0)
    acc0_out[...] = acc[...]
    write_dq(dqt, 1, beside_ref)


def own_kernel(
    place_ref, ranges, dqt_in, lse_ref, delta_ref, tops, weights, qg_all, kv_all, acc0,
    dqt, dq_ref, dkv_ref, acc,
):
    del dqt_in
    acc[...] = acc0[...]
    visit_step(
        place_ref[1], jnp.int32(0), (0, 1), ranges,
        (lse_ref, delta_ref, tops, weights, qg_all, kv_all), dqt, acc,
    )
    write_dkv(dkv_ref, acc)
    write_dq(dqt, 0, dq_ref)


def pair_kernel(keep, got, out_ref):
    out_ref[...] = (keep[...].astype(F32) + got[...].astype(F32)).astype(BF16)


def merge_kernel(keep, beside, across, dkv0, got1, got2, got4, got5, out_ref):
    parts, part = out_ref.shape[:2]
    width = GROUP * HD
    dkv = dkv0[...] + got1[...].astype(F32) + got2[...].astype(F32)
    dkv = dkv + got4[...].astype(F32) + got5[...].astype(F32)
    dq = keep[...].astype(F32) + beside[...].astype(F32) + across[...].astype(F32)
    out_ref[:, :, :width] = dq.astype(BF16).reshape(parts, part, width)
    out_ref[:, :, width:] = dkv.astype(BF16).reshape(parts, part, 2 * HD)


def finish_kernel(got, q_ref, k_ref, v_ref):
    width = GROUP * HD
    for t in range(got.shape[0]):
        q_ref[:, t * width : (t + 1) * width] = got[t, :, :width]
        k_ref[:, t * HD : (t + 1) * HD] = got[t, :, width : width + HD]
        v_ref[:, t * HD : (t + 1) * HD] = got[t, :, width + HD :]


SMEM_SPEC = pl.BlockSpec(memory_space=pltpu.SMEM)
VMEM_SPEC = pl.BlockSpec(memory_space=pltpu.VMEM)


def call(kernel, name, outs, scratch, *args, scalars=2, aliases=None, smem_outs=0):
    return pl.pallas_call(
        kernel,
        out_shape=tuple(jax.ShapeDtypeStruct(shape, dtype) for shape, dtype in outs),
        in_specs=[SMEM_SPEC] * scalars + [VMEM_SPEC] * (len(args) - scalars),
        out_specs=(SMEM_SPEC,) * smem_outs + (VMEM_SPEC,) * (len(outs) - smem_outs),
        scratch_shapes=[pltpu.VMEM(shape, dtype) for shape, dtype in scratch],
        input_output_aliases=aliases or {},
        compiler_params=pltpu.CompilerParams(vmem_limit_bytes=VMEM_LIMIT),
        cost_estimate=pl.CostEstimate(flops=1, bytes_accessed=1, transcendentals=0),
        name=name,
    )(*args)


QG_ALL = ((SLAB, ROWS, 2 * GROUP * HD), BF16)
KV_ALL = ((REACH + 1, ROWS, 2 * HD), BF16)
STATS = ((3, SLAB * GROUP, ROWS), F32)
TOPS = ((REACH + 1, SLAB * GROUP, ROWS), F32)
WEIGHTS = ((SLAB * (REACH + 1), GROUP, ROWS, ROWS), BF16)
RANGES = ((2 * SLAB,), jnp.int32)
STARTS = ((2 * SLAB, ROWS), jnp.int32)
ROW_STATS = ((SLAB * GROUP, ROWS), F32)
DQT = ((SLAB * GROUP, HD, ROWS), F32)
ACC = ((ROWS, 2 * HD), F32)
DKV = ((ROWS, 2 * HD), BF16)
DQ = ((ROWS, GROUP * HD), BF16)


def flip(x, axis):
    return lax.ppermute(x, axis, [(0, 1), (1, 0)])


def shift(x, by, slabs):
    pairs = [(i, i + by) for i in range(slabs) if 0 <= i + by < slabs]
    return lax.ppermute(x, "z", pairs)


def wrapped(x, by, sources, slabs):
    return lax.ppermute(x, "z", [(i, (i + by) % slabs) for i in sources])


def crossed(x, by, slabs):
    pairs = [
        (i * SLAB + at, (i + by) * SLAB + (at ^ 1))
        for i in range(slabs)
        if 0 <= i + by < slabs
        for at in range(SLAB)
    ]
    return flip(lax.ppermute(x, ("z", "y", "core"), pairs), "core")


def shift_last(x, by, slabs):
    last = SLAB - 1
    pairs = [
        (i * SLAB + last, (i + by) * SLAB + last) for i in range(slabs) if 0 <= i + by < slabs
    ]
    return lax.ppermute(x, ("z", "y", "core"), pairs)


def local(queries, keys, values, grad_out, doc_lengths):
    z = lax.axis_index("z")
    j = lax.axis_index(("y", "core"))
    slabs = lax.axis_size("z")
    place = jnp.stack((z, j)).astype(jnp.int32)

    qg, kv = pl.pallas_call(
        pack_kernel,
        out_shape=(
            jax.ShapeDtypeStruct((ROWS, 2 * GROUP * HD), BF16),
            jax.ShapeDtypeStruct((ROWS, 2 * HD), BF16),
        ),
        in_specs=[pl.BlockSpec(memory_space=pltpu.HBM)] * 4,
        out_specs=(VMEM_SPEC,) * 2,
        scratch_shapes=[pltpu.SemaphoreType.DMA((4,))],
        compiler_params=pltpu.CompilerParams(vmem_limit_bytes=56 * 1024 * 1024),
        cost_estimate=pl.CostEstimate(flops=1, bytes_accessed=1, transcendentals=0),
        name="pack",
    )(queries, grad_out, keys, values)
    across = flip(qg, "y")
    ahead = [i for i in range(slabs) if i + 4 < slabs]
    kv_by = wrapped(kv, -2, ahead, slabs)
    kv5 = shift_last(kv, 5, slabs)
    kv1 = shift(kv, 1, slabs)
    kv2 = shift(kv, 2, slabs)
    beside = flip(qg, "core")

    ranges, starts, stats, tops, weights, qg_all, kv_all = call(
        first_stats_kernel, "first_statistics",
        [RANGES, STARTS, STATS, TOPS, WEIGHTS, QG_ALL, KV_ALL], [],
        place, doc_lengths, qg, beside, kv, smem_outs=1,
    )
    across, kv_by, kv5, kv1, kv2, stats = lax.optimization_barrier(
        (across, kv_by, kv5, kv1, kv2, stats)
    )
    kv3 = shift(kv2, 1, slabs)
    kv4 = wrapped(kv_by, -2, [(i - 2) % slabs for i in ahead], slabs)
    both = flip(across, "core")
    stats, tops, weights, kv_all = call(
        here_stats_kernel, "here_statistics", [STATS, TOPS, WEIGHTS, KV_ALL], [],
        place, ranges, stats, tops, weights, kv_all, starts, qg_all, kv1, kv2,
        aliases={2: 0, 3: 1, 4: 2, 5: 3},
    )
    stats, tops, weights, qg_all = call(
        there_stats_kernel, "there_statistics", [STATS, TOPS, WEIGHTS, QG_ALL], [],
        place, ranges, stats, tops, weights, qg_all, starts, kv_all, across, both,
        aliases={2: 0, 3: 1, 4: 2, 5: 3},
    )
    stats, tops, weights, kv_all = call(
        far_stats_kernel, "far_statistics", [STATS, TOPS, WEIGHTS, KV_ALL], [],
        place, ranges, stats, tops, weights, kv_all, starts, qg_all, kv3, kv4, kv5,
        aliases={2: 0, 3: 1, 4: 2, 5: 3},
    )
    stats_y = flip(stats, "y")
    stats_c = flip(stats, "core")
    stats_yc = flip(stats_y, "core")

    data = (tops, weights, qg_all, kv_all)
    dqt, dkv3, dkv4, dkv5, acc0, lse, delta = call(
        far_kernel, "far_gradients", [DQT, DKV, DKV, DKV, ACC, ROW_STATS, ROW_STATS], [ACC],
        place, ranges, stats, stats_c, stats_y, stats_yc, *data,
    )
    got3 = shift(dkv3, -2, slabs)
    got4 = crossed(dkv4, -4, slabs)
    got5 = shift_last(dkv5, -5, slabs)
    dqt, there_keep, there_send, acc_near = call(
        there_kernel, "there_gradients", [DQT, DQ, DQ, ((2,) + ACC[0], F32)], [ACC],
        place, ranges, dqt, lse, delta, *data, aliases={2: 0},
    )
    there_got = flip(there_send, "core")
    dqt, dq_beside, dkv1, dkv2, acc0 = call(
        here_kernel, "here_gradients", [DQT, DQ, ACC, DKV, ACC], [ACC],
        place, ranges, dqt, lse, delta, *data, acc0, acc_near, aliases={2: 0},
    )
    dkv1 = (dkv1 + got3.astype(F32)).astype(BF16)
    there_got, dkv1 = lax.optimization_barrier((there_got, dkv1))
    dq_pair, = call(
        pair_kernel, "pair", [DQ], [], there_keep, there_got, scalars=0
    )
    dq_across = flip(dq_pair, "y")
    dq_beside = flip(dq_beside, "core")
    got2 = shift(dkv2, -2, slabs)
    got1 = shift(dkv1, -1, slabs)
    _, dq_keep, dkv0 = call(
        own_kernel, "own_gradients", [DQT, DQ, ACC], [ACC],
        place, ranges, dqt, lse, delta, *data, acc0, aliases={2: 0},
    )

    tp = lax.axis_size("tp")
    part = ROWS // tp
    width = GROUP * HD
    whole, = call(
        merge_kernel, "merge", [((tp, part, width + 2 * HD), BF16)], [],
        dq_keep, dq_beside, dq_across, dkv0, got1, got2, got4, got5, scalars=0,
    )
    got = lax.all_to_all(whole, "tp", split_axis=0, concat_axis=0, tiled=True)
    return call(
        finish_kernel, "finish",
        [((part, tp * width), BF16), ((part, tp * HD), BF16), ((part, tp * HD), BF16)], [],
        got, scalars=0,
    )


def solution(mesh):
    tp = mesh.shape["tp"]
    inner = Mesh(mesh.devices.reshape(-1, 2, 2, tp), ("z", "y", "core", "tp"))
    tokens = ("z", "y", "core")
    in_specs = (P(tokens, "tp"),) * 4 + (P(),)
    out_specs = (P(tokens + ("tp",), None),) * 3
    return jax.shard_map(local, mesh=inner, in_specs=in_specs, out_specs=out_specs, check_vma=False)
```

```python
import math

import jax
import jax.numpy as jnp
from jax import lax
from jax.experimental import pallas as pl
from jax.experimental.pallas import tpu as pltpu
from jax.sharding import Mesh, PartitionSpec as P

HD = 128
GROUP = 4
ROWS = 256
SLAB = 4
REACH = 5
HALF = 3
HERE = (0, 2)
THERE = (2, 4)
DOC_COUNT = 17
SCALE = HD ** -0.5
SCALE2 = SCALE * math.log2(math.e)
MASKED = -1e30
EMPTY = -1e29
VMEM_LIMIT = 16 * 1024 * 1024
NT = (((1,), (1,)), ((), ()))
NN = (((1,), (0,)), ((), ()))
F32 = jnp.float32
BF16 = jnp.bfloat16


def dot_nt(a, b):
    return lax.dot_general(a, b, NT, preferred_element_type=F32)


def dot_nn(a, b):
    return lax.dot_general(a, b, NN, preferred_element_type=F32)


def start_of(doc_ref, positions):
    end = jnp.int32(0)
    starts = jnp.zeros_like(positions)
    for doc in range(DOC_COUNT):
        length = doc_ref[doc]
        end = end + length
        starts = starts + jnp.where(end <= positions, length, 0)
    return starts


def find_starts(place_ref, doc_ref, starts_ref, ranges_ref):
    z, j = place_ref[0], place_ref[1]
    for rel in range(SLAB):
        qb = j ^ rel
        first = start_of(doc_ref, (SLAB * z + qb) * ROWS) // ROWS
        ranges_ref[2 * rel] = jnp.where(j <= qb, 0, 1)
        ranges_ref[2 * rel + 1] = z - jnp.maximum((first - j + SLAB - 1) >> 2, 0)
        starts_ref[rel : rel + 1, :] = start_of(doc_ref, query_positions(z, qb))


def query_positions(z, qb):
    return (SLAB * z + qb) * ROWS + lax.broadcasted_iota(jnp.int32, (1, ROWS), 1)


def pack_kernel(q_ref, g_ref, k_ref, v_ref, qg_ref, kv_ref, sems):
    wide, thin = GROUP * HD, HD
    copies = [
        pltpu.make_async_copy(k_ref, kv_ref.at[:, :thin], sems.at[0]),
        pltpu.make_async_copy(v_ref, kv_ref.at[:, thin:], sems.at[1]),
        pltpu.make_async_copy(q_ref, qg_ref.at[:, :wide], sems.at[2]),
        pltpu.make_async_copy(g_ref, qg_ref.at[:, wide:], sems.at[3]),
    ]
    for copy in copies:
        copy.start()
    for copy in copies:
        copy.wait()


def stats_steps(place_ref, where, rels, steps, fresh, qg, kv, tops, weights, out_ref):
    z, j = place_ref[0], place_ref[1]
    ranges, starts_ref = where

    def per_block(rel, _):
        qb = j ^ rel
        positions = query_positions(z, qb)
        starts = starts_ref[pl.ds(rel, 1), :]

        def per_step(k, carry):
            key_pos = lax.broadcasted_iota(jnp.int32, (ROWS, ROWS), 0)
            offset = (SLAB * (z - k) + j) * ROWS
            mask = (key_pos >= starts - offset) & (key_pos <= positions - offset)
            keys = kv[k, :, :HD]
            values = kv[k, :, HD:]

            def products(h):
                q = qg[rel, :, h * HD : (h + 1) * HD]
                g = qg[rel, :, (GROUP + h) * HD : (GROUP + h + 1) * HD]
                return dot_nt(keys, q), dot_nt(values, g)

            new = []
            ahead = products(0)
            for h in range(GROUP):
                s, dp = ahead
                if h + 1 < GROUP:
                    ahead = products(h + 1)
                top, total, dot = carry[3 * h : 3 * h + 3]
                s = jnp.where(mask, s * SCALE2, MASKED)
                new_top = jnp.maximum(top, jnp.max(s, axis=0, keepdims=True))
                p = jnp.exp2(s - new_top)
                weights[rel * (REACH + 1) + k, h] = p.astype(BF16)
                tops[k, pl.ds(rel * GROUP + h, 1), :] = new_top
                factor = jnp.exp2(top - new_top)
                new += [
                    new_top,
                    total * factor + jnp.sum(p, axis=0, keepdims=True),
                    dot * factor + jnp.sum(p * dp, axis=0, keepdims=True),
                ]
            return tuple(new)

        if fresh:
            zero = jnp.zeros((1, ROWS), F32)
            init = (jnp.full((1, ROWS), EMPTY, F32), zero, zero) * GROUP
        else:
            init = tuple(
                out_ref[part, pl.ds(qb * GROUP + h, 1), :]
                for h in range(GROUP)
                for part in range(3)
            )
        first = jnp.maximum(ranges[2 * rel], steps[0])
        end = jnp.minimum(ranges[2 * rel + 1] + 1, steps[1])
        done = lax.fori_loop(first, end, per_step, init)
        for h in range(GROUP):
            for part in range(3):
                out_ref[part, pl.ds(qb * GROUP + h, 1), :] = done[3 * h + part]
        return 0

    lax.fori_loop(rels[0], rels[1], per_block, 0)


def first_stats_kernel(
    place_ref, doc_ref, qg0, qg1, kv0, ranges, starts, out_ref, tops, weights, qg_all, kv_all
):
    find_starts(place_ref, doc_ref, starts, ranges)
    qg_all[0] = qg0[...]
    qg_all[1] = qg1[...]
    kv_all[0] = kv0[...]
    stats_steps(
        place_ref, (ranges, starts), HERE, (0, 1), True, qg_all, kv_all, tops, weights, out_ref
    )


def here_stats_kernel(
    place_ref, ranges, in0, in1, in2, in3, starts, qg_all, kv1, kv2, out_ref, tops, weights, kv_all
):
    del in0, in1, in2, in3
    kv_all[1] = kv1[...]
    kv_all[2] = kv2[...]
    stats_steps(
        place_ref, (ranges, starts), HERE, (1, HALF), False,
        qg_all, kv_all, tops, weights, out_ref,
    )


def there_stats_kernel(
    place_ref, ranges, in0, in1, in2, in3, starts, kv_all, qg2, qg3, out_ref, tops, weights, qg_all
):
    del in0, in1, in2, in3
    qg_all[2] = qg2[...]
    qg_all[3] = qg3[...]
    stats_steps(
        place_ref, (ranges, starts), THERE, (0, HALF), True,
        qg_all, kv_all, tops, weights, out_ref,
    )


def far_stats_kernel(
    place_ref, ranges, in0, in1, in2, in3, starts, qg_all, kv3, kv4, kv5,
    out_ref, tops, weights, kv_all,
):
    del in0, in1, in2, in3
    for slot, ref in enumerate((kv3, kv4, kv5)):
        kv_all[HALF + slot] = ref[...]
    stats_steps(
        place_ref, (ranges, starts), (0, SLAB), (HALF, REACH + 1), False,
        qg_all, kv_all, tops, weights, out_ref,
    )


def combine_stats(st_refs, lse_buf, delta_buf):
    stats = [ref[...] for ref in st_refs]
    top = jnp.maximum(
        jnp.maximum(stats[0][0], stats[1][0]), jnp.maximum(stats[2][0], stats[3][0])
    )
    total = jnp.zeros_like(top)
    dot = jnp.zeros_like(top)
    for st in stats:
        factor = jnp.exp2(st[0] - top)
        total = total + st[1] * factor
        dot = dot + st[2] * factor
    lse_buf[...] = top + jnp.log2(total)
    delta_buf[...] = dot / total


def visit_step(j, k, rels, ranges, data, dqt, acc):
    lse_buf, delta_buf, tops, weights, qg_all, kv_all = data
    keys_t = kv_all[k, :, :HD].T

    def per_block(rel, _):
        qb = j ^ rel

        @pl.when((k >= ranges[2 * rel]) & (k <= ranges[2 * rel + 1]))
        def _():
            values = kv_all[k, :, HD:]

            def grad_of(h):
                return qg_all[rel, :, (GROUP + h) * HD : (GROUP + h + 1) * HD]

            dk = dv = None
            ahead = dot_nt(values, grad_of(0))
            for h in range(GROUP):
                dp = ahead
                if h + 1 < GROUP:
                    ahead = dot_nt(values, grad_of(h + 1))
                q = qg_all[rel, :, h * HD : (h + 1) * HD]
                lse = lse_buf[pl.ds(qb * GROUP + h, 1), :]
                delta = delta_buf[pl.ds(qb * GROUP + h, 1), :]
                factor = jnp.exp2(tops[k, pl.ds(rel * GROUP + h, 1), :] - lse)
                p = weights[rel * (REACH + 1) + k, h].astype(F32) * factor
                ds = p * (dp - delta)
                pb = p.astype(BF16)
                dsb = ds.astype(BF16)
                dv_add, dk_add = dot_nn(pb, grad_of(h)), dot_nn(dsb, q)
                dv = dv_add if dv is None else dv + dv_add
                dk = dk_add if dk is None else dk + dk_add
                dqt[rel * GROUP + h] += dot_nn(keys_t, dsb)
            acc[:, :HD] += dk
            acc[:, HD:] += dv

        return 0

    lax.fori_loop(rels[0], rels[1], per_block, 0)


def write_dq(dqt, slot, out_ref):
    for h in range(GROUP):
        dq = (dqt[slot * GROUP + h] * SCALE).astype(BF16)
        out_ref[:, h * HD : (h + 1) * HD] = dq.T


def write_dkv(out_ref, acc):
    out_ref[:, :HD] = (acc[:, :HD] * SCALE).astype(out_ref.dtype)
    out_ref[:, HD:] = acc[:, HD:].astype(out_ref.dtype)


def far_kernel(
    place_ref, ranges, st0, st1, st2, st3, tops, weights, qg_all, kv_all,
    dqt, dkv3, dkv4, dkv5, acc0_ref, lse_ref, delta_ref, acc,
):
    combine_stats((st0, st1, st2, st3), lse_ref, delta_ref)
    dqt[...] = jnp.zeros_like(dqt)

    def per_step(step, _):
        k = jnp.where(step == 0, 0, REACH + 1 - step)
        acc[...] = jnp.zeros_like(acc)
        visit_step(
            place_ref[1], k, (jnp.where(step == 0, THERE[0], 0), SLAB), ranges,
            (lse_ref, delta_ref, tops, weights, qg_all, kv_all), dqt, acc,
        )

        @pl.when(step == 0)
        def _():
            acc0_ref[...] = acc[...]

        for slot, ref in enumerate((dkv5, dkv4, dkv3)):

            @pl.when(step == slot + 1)
            def _():
                write_dkv(ref, acc)

        return 0

    lax.fori_loop(0, HALF + 1, per_step, 0)


def there_kernel(
    place_ref, ranges, dqt_in, lse_ref, delta_ref, tops, weights, qg_all, kv_all,
    dqt, keep_ref, send_ref, acc_ref, acc,
):
    del dqt_in

    def per_step(step, _):
        k = 2 - step
        acc[...] = jnp.zeros_like(acc)
        visit_step(
            place_ref[1], k, THERE, ranges,
            (lse_ref, delta_ref, tops, weights, qg_all, kv_all), dqt, acc,
        )
        acc_ref[k - 1] = acc[...]
        return 0

    lax.fori_loop(0, 2, per_step, 0)
    write_dq(dqt, 2, keep_ref)
    write_dq(dqt, 3, send_ref)


def here_kernel(
    place_ref, ranges, dqt_in, lse_ref, delta_ref, tops, weights, qg_all, kv_all, acc0, acc_near,
    dqt, beside_ref, dkv1, dkv2, acc0_out, acc,
):
    del dqt_in

    def per_step(step, _):
        k = 2 - step

        @pl.when(k > 0)
        def _():
            acc[...] = acc_near[jnp.maximum(k - 1, 0)]

        @pl.when(k == 0)
        def _():
            acc[...] = acc0[...]

        visit_step(
            place_ref[1], k, (jnp.where(k == 0, 1, 0), HERE[1]), ranges,
            (lse_ref, delta_ref, tops, weights, qg_all, kv_all), dqt, acc,
        )

        @pl.when(k == 2)
        def _():
            write_dkv(dkv2, acc)

        @pl.when(k == 1)
        def _():
            write_dkv(dkv1, acc)

        return 0

    lax.fori_loop(0, 3, per_step, 0)
    acc0_out[...] = acc[...]
    write_dq(dqt, 1, beside_ref)


def own_kernel(
    place_ref, ranges, dqt_in, lse_ref, delta_ref, tops, weights, qg_all, kv_all, acc0,
    dqt, dq_ref, dkv_ref, acc,
):
    del dqt_in
    acc[...] = acc0[...]
    visit_step(
        place_ref[1], jnp.int32(0), (0, 1), ranges,
        (lse_ref, delta_ref, tops, weights, qg_all, kv_all), dqt, acc,
    )
    write_dkv(dkv_ref, acc)
    write_dq(dqt, 0, dq_ref)


def pair_kernel(keep, got, out_ref):
    out_ref[...] = (keep[...].astype(F32) + got[...].astype(F32)).astype(BF16)


def merge_kernel(keep, beside, across, dkv0, got1, got2, got4, got5, out_ref):
    parts, part = out_ref.shape[:2]
    width = GROUP * HD
    dkv = dkv0[...] + got1[...].astype(F32) + got2[...].astype(F32)
    dkv = dkv + got4[...].astype(F32) + got5[...].astype(F32)
    dq = keep[...].astype(F32) + beside[...].astype(F32) + across[...].astype(F32)
    out_ref[:, :, :width] = dq.astype(BF16).reshape(parts, part, width)
    out_ref[:, :, width:] = dkv.astype(BF16).reshape(parts, part, 2 * HD)


def finish_kernel(got, q_ref, k_ref, v_ref):
    width = GROUP * HD
    for t in range(got.shape[0]):
        q_ref[:, t * width : (t + 1) * width] = got[t, :, :width]
        k_ref[:, t * HD : (t + 1) * HD] = got[t, :, width : width + HD]
        v_ref[:, t * HD : (t + 1) * HD] = got[t, :, width + HD :]


SMEM_SPEC = pl.BlockSpec(memory_space=pltpu.SMEM)
VMEM_SPEC = pl.BlockSpec(memory_space=pltpu.VMEM)


def call(kernel, name, outs, scratch, *args, scalars=2, aliases=None, smem_outs=0):
    return pl.pallas_call(
        kernel,
        out_shape=tuple(jax.ShapeDtypeStruct(shape, dtype) for shape, dtype in outs),
        in_specs=[SMEM_SPEC] * scalars + [VMEM_SPEC] * (len(args) - scalars),
        out_specs=(SMEM_SPEC,) * smem_outs + (VMEM_SPEC,) * (len(outs) - smem_outs),
        scratch_shapes=[pltpu.VMEM(shape, dtype) for shape, dtype in scratch],
        input_output_aliases=aliases or {},
        compiler_params=pltpu.CompilerParams(vmem_limit_bytes=VMEM_LIMIT),
        cost_estimate=pl.CostEstimate(flops=1, bytes_accessed=1, transcendentals=0),
        name=name,
    )(*args)


QG_ALL = ((SLAB, ROWS, 2 * GROUP * HD), BF16)
KV_ALL = ((REACH + 1, ROWS, 2 * HD), BF16)
STATS = ((3, SLAB * GROUP, ROWS), F32)
TOPS = ((REACH + 1, SLAB * GROUP, ROWS), F32)
WEIGHTS = ((SLAB * (REACH + 1), GROUP, ROWS, ROWS), BF16)
RANGES = ((2 * SLAB,), jnp.int32)
STARTS = ((2 * SLAB, ROWS), jnp.int32)
ROW_STATS = ((SLAB * GROUP, ROWS), F32)
DQT = ((SLAB * GROUP, HD, ROWS), F32)
ACC = ((ROWS, 2 * HD), F32)
DKV = ((ROWS, 2 * HD), BF16)
DQ = ((ROWS, GROUP * HD), BF16)


def flip(x, axis):
    return lax.ppermute(x, axis, [(0, 1), (1, 0)])


def shift(x, by, slabs):
    pairs = [(i, i + by) for i in range(slabs) if 0 <= i + by < slabs]
    return lax.ppermute(x, "z", pairs)


def wrapped(x, by, sources, slabs):
    return lax.ppermute(x, "z", [(i, (i + by) % slabs) for i in sources])


def shift_last(x, by, slabs):
    last = SLAB - 1
    pairs = [
        (i * SLAB + last, (i + by) * SLAB + last) for i in range(slabs) if 0 <= i + by < slabs
    ]
    return lax.ppermute(x, ("z", "y", "core"), pairs)


def local(queries, keys, values, grad_out, doc_lengths):
    z = lax.axis_index("z")
    j = lax.axis_index(("y", "core"))
    slabs = lax.axis_size("z")
    place = jnp.stack((z, j)).astype(jnp.int32)

    qg, kv = pl.pallas_call(
        pack_kernel,
        out_shape=(
            jax.ShapeDtypeStruct((ROWS, 2 * GROUP * HD), BF16),
            jax.ShapeDtypeStruct((ROWS, 2 * HD), BF16),
        ),
        in_specs=[pl.BlockSpec(memory_space=pltpu.HBM)] * 4,
        out_specs=(VMEM_SPEC,) * 2,
        scratch_shapes=[pltpu.SemaphoreType.DMA((4,))],
        compiler_params=pltpu.CompilerParams(vmem_limit_bytes=56 * 1024 * 1024),
        cost_estimate=pl.CostEstimate(flops=1, bytes_accessed=1, transcendentals=0),
        name="pack",
    )(queries, grad_out, keys, values)
    across = flip(qg, "y")
    ahead = [i for i in range(slabs) if i + 4 < slabs]
    kv_by = wrapped(kv, -2, ahead, slabs)
    kv5 = shift_last(kv, 5, slabs)
    kv1 = shift(kv, 1, slabs)
    kv2 = shift(kv, 2, slabs)
    beside = flip(qg, "core")

    ranges, starts, stats, tops, weights, qg_all, kv_all = call(
        first_stats_kernel, "first_statistics",
        [RANGES, STARTS, STATS, TOPS, WEIGHTS, QG_ALL, KV_ALL], [],
        place, doc_lengths, qg, beside, kv, smem_outs=1,
    )
    across, kv_by, kv5, kv1, kv2, stats = lax.optimization_barrier(
        (across, kv_by, kv5, kv1, kv2, stats)
    )
    kv3 = shift(kv2, 1, slabs)
    kv4 = wrapped(kv_by, -2, [(i - 2) % slabs for i in ahead], slabs)
    both = flip(across, "core")
    stats, tops, weights, kv_all = call(
        here_stats_kernel, "here_statistics", [STATS, TOPS, WEIGHTS, KV_ALL], [],
        place, ranges, stats, tops, weights, kv_all, starts, qg_all, kv1, kv2,
        aliases={2: 0, 3: 1, 4: 2, 5: 3},
    )
    stats, tops, weights, qg_all = call(
        there_stats_kernel, "there_statistics", [STATS, TOPS, WEIGHTS, QG_ALL], [],
        place, ranges, stats, tops, weights, qg_all, starts, kv_all, across, both,
        aliases={2: 0, 3: 1, 4: 2, 5: 3},
    )
    stats, tops, weights, kv_all = call(
        far_stats_kernel, "far_statistics", [STATS, TOPS, WEIGHTS, KV_ALL], [],
        place, ranges, stats, tops, weights, kv_all, starts, qg_all, kv3, kv4, kv5,
        aliases={2: 0, 3: 1, 4: 2, 5: 3},
    )
    stats_y = flip(stats, "y")
    stats_c = flip(stats, "core")
    stats_yc = flip(stats_y, "core")

    data = (tops, weights, qg_all, kv_all)
    dqt, dkv3, dkv4, dkv5, acc0, lse, delta = call(
        far_kernel, "far_gradients", [DQT, DKV, DKV, DKV, ACC, ROW_STATS, ROW_STATS], [ACC],
        place, ranges, stats, stats_c, stats_y, stats_yc, *data,
    )
    got3 = shift(dkv3, -2, slabs)
    far_slabs = [i for i in range(slabs) if i >= 4]
    got4 = wrapped(dkv4, 2, far_slabs, slabs)
    got5 = shift_last(dkv5, -5, slabs)
    dqt, there_keep, there_send, acc_near = call(
        there_kernel, "there_gradients", [DQT, DQ, DQ, ((2,) + ACC[0], F32)], [ACC],
        place, ranges, dqt, lse, delta, *data, aliases={2: 0},
    )
    there_got = flip(there_send, "core")
    dqt, dq_beside, dkv1, dkv2, acc0 = call(
        here_kernel, "here_gradients", [DQT, DQ, ACC, DKV, ACC], [ACC],
        place, ranges, dqt, lse, delta, *data, acc0, acc_near, aliases={2: 0},
    )
    dkv1 = (dkv1 + got3.astype(F32)).astype(BF16)
    there_got, dkv1 = lax.optimization_barrier((there_got, dkv1))
    dq_pair, = call(
        pair_kernel, "pair", [DQ], [], there_keep, there_got, scalars=0
    )
    dq_across = flip(dq_pair, "y")
    dq_beside = flip(dq_beside, "core")
    got4 = wrapped(got4, 2, [(i + 2) % slabs for i in far_slabs], slabs)
    got2 = shift(dkv2, -2, slabs)
    got1 = shift(dkv1, -1, slabs)
    _, dq_keep, dkv0 = call(
        own_kernel, "own_gradients", [DQT, DQ, ACC], [ACC],
        place, ranges, dqt, lse, delta, *data, acc0, aliases={2: 0},
    )

    tp = lax.axis_size("tp")
    part = ROWS // tp
    width = GROUP * HD
    whole, = call(
        merge_kernel, "merge", [((tp, part, width + 2 * HD), BF16)], [],
        dq_keep, dq_beside, dq_across, dkv0, got1, got2, got4, got5, scalars=0,
    )
    got = lax.all_to_all(whole, "tp", split_axis=0, concat_axis=0, tiled=True)
    return call(
        finish_kernel, "finish",
        [((part, tp * width), BF16), ((part, tp * HD), BF16), ((part, tp * HD), BF16)], [],
        got, scalars=0,
    )


def solution(mesh):
    tp = mesh.shape["tp"]
    inner = Mesh(mesh.devices.reshape(-1, 2, 2, tp), ("z", "y", "core", "tp"))
    tokens = ("z", "y", "core")
    in_specs = (P(tokens, "tp"),) * 4 + (P(),)
    out_specs = (P(tokens + ("tp",), None),) * 3
    return jax.shard_map(local, mesh=inner, in_specs=in_specs, out_specs=out_specs, check_vma=False)
```

```python
import math

import jax
import jax.numpy as jnp
from jax import lax
from jax.experimental import pallas as pl
from jax.experimental.pallas import tpu as pltpu
from jax.sharding import Mesh, PartitionSpec as P

HD = 128
GROUP = 4
ROWS = 256
SLAB = 4
REACH = 5
HALF = 3
HERE = (0, 2)
THERE = (2, 4)
DOC_COUNT = 17
SCALE = HD ** -0.5
SCALE2 = SCALE * math.log2(math.e)
MASKED = -1e30
EMPTY = -1e29
VMEM_LIMIT = 16 * 1024 * 1024
NT = (((1,), (1,)), ((), ()))
NN = (((1,), (0,)), ((), ()))
F32 = jnp.float32
BF16 = jnp.bfloat16


def dot_nt(a, b):
    return lax.dot_general(a, b, NT, preferred_element_type=F32)


def dot_nn(a, b):
    return lax.dot_general(a, b, NN, preferred_element_type=F32)


def start_of(doc_ref, positions):
    end = jnp.int32(0)
    starts = jnp.zeros_like(positions)
    for doc in range(DOC_COUNT):
        length = doc_ref[doc]
        end = end + length
        starts = starts + jnp.where(end <= positions, length, 0)
    return starts


def find_starts(place_ref, doc_ref, starts_ref, ranges_ref):
    z, j = place_ref[0], place_ref[1]
    for rel in range(SLAB):
        qb = j ^ rel
        first = start_of(doc_ref, (SLAB * z + qb) * ROWS) // ROWS
        ranges_ref[2 * rel] = jnp.where(j <= qb, 0, 1)
        ranges_ref[2 * rel + 1] = z - jnp.maximum((first - j + SLAB - 1) >> 2, 0)
        starts_ref[rel : rel + 1, :] = start_of(doc_ref, query_positions(z, qb))


def query_positions(z, qb):
    return (SLAB * z + qb) * ROWS + lax.broadcasted_iota(jnp.int32, (1, ROWS), 1)


def pack_kernel(q_ref, g_ref, k_ref, v_ref, qg_ref, kv_ref, sems):
    wide, thin = GROUP * HD, HD
    copies = [
        pltpu.make_async_copy(k_ref, kv_ref.at[:, :thin], sems.at[0]),
        pltpu.make_async_copy(v_ref, kv_ref.at[:, thin:], sems.at[1]),
        pltpu.make_async_copy(q_ref, qg_ref.at[:, :wide], sems.at[2]),
        pltpu.make_async_copy(g_ref, qg_ref.at[:, wide:], sems.at[3]),
    ]
    for copy in copies:
        copy.start()
    for copy in copies:
        copy.wait()


def stats_steps(place_ref, where, rels, steps, fresh, qg, kv, tops, weights, out_ref):
    z, j = place_ref[0], place_ref[1]
    ranges, starts_ref = where

    def per_block(rel, _):
        qb = j ^ rel
        positions = query_positions(z, qb)
        starts = starts_ref[pl.ds(rel, 1), :]

        def per_step(k, carry):
            key_pos = lax.broadcasted_iota(jnp.int32, (ROWS, ROWS), 0)
            offset = (SLAB * (z - k) + j) * ROWS
            mask = (key_pos >= starts - offset) & (key_pos <= positions - offset)
            keys = kv[k, :, :HD]
            values = kv[k, :, HD:]

            def products(h):
                q = qg[rel, :, h * HD : (h + 1) * HD]
                g = qg[rel, :, (GROUP + h) * HD : (GROUP + h + 1) * HD]
                return dot_nt(keys, q), dot_nt(values, g)

            new = []
            ahead = products(0)
            for h in range(GROUP):
                s, dp = ahead
                if h + 1 < GROUP:
                    ahead = products(h + 1)
                top, total, dot = carry[3 * h : 3 * h + 3]
                s = jnp.where(mask, s * SCALE2, MASKED)
                new_top = jnp.maximum(top, jnp.max(s, axis=0, keepdims=True))
                p = jnp.exp2(s - new_top)
                weights[rel * (REACH + 1) + k, h] = p.astype(BF16)
                tops[k, pl.ds(rel * GROUP + h, 1), :] = new_top
                factor = jnp.exp2(top - new_top)
                new += [
                    new_top,
                    total * factor + jnp.sum(p, axis=0, keepdims=True),
                    dot * factor + jnp.sum(p * dp, axis=0, keepdims=True),
                ]
            return tuple(new)

        if fresh:
            zero = jnp.zeros((1, ROWS), F32)
            init = (jnp.full((1, ROWS), EMPTY, F32), zero, zero) * GROUP
        else:
            init = tuple(
                out_ref[part, pl.ds(qb * GROUP + h, 1), :]
                for h in range(GROUP)
                for part in range(3)
            )
        first = jnp.maximum(ranges[2 * rel], steps[0])
        end = jnp.minimum(ranges[2 * rel + 1] + 1, steps[1])
        done = lax.fori_loop(first, end, per_step, init)
        for h in range(GROUP):
            for part in range(3):
                out_ref[part, pl.ds(qb * GROUP + h, 1), :] = done[3 * h + part]
        return 0

    lax.fori_loop(rels[0], rels[1], per_block, 0)


def first_stats_kernel(
    place_ref, doc_ref, qg0, qg1, kv0, ranges, starts, out_ref, tops, weights, qg_all, kv_all
):
    find_starts(place_ref, doc_ref, starts, ranges)
    qg_all[0] = qg0[...]
    qg_all[1] = qg1[...]
    kv_all[0] = kv0[...]
    stats_steps(
        place_ref, (ranges, starts), HERE, (0, 1), True, qg_all, kv_all, tops, weights, out_ref
    )


def here_stats_kernel(
    place_ref, ranges, in0, in1, in2, in3, starts, qg_all, kv1, kv2, out_ref, tops, weights, kv_all
):
    del in0, in1, in2, in3
    kv_all[1] = kv1[...]
    kv_all[2] = kv2[...]
    stats_steps(
        place_ref, (ranges, starts), HERE, (1, HALF), False,
        qg_all, kv_all, tops, weights, out_ref,
    )


def there_stats_kernel(
    place_ref, ranges, in0, in1, in2, in3, starts, kv_all, qg2, qg3, out_ref, tops, weights, qg_all
):
    del in0, in1, in2, in3
    qg_all[2] = qg2[...]
    qg_all[3] = qg3[...]
    stats_steps(
        place_ref, (ranges, starts), THERE, (0, HALF), True,
        qg_all, kv_all, tops, weights, out_ref,
    )


def far_stats_kernel(
    place_ref, ranges, in0, in1, in2, in3, starts, qg_all, kv3, kv4, kv5,
    out_ref, tops, weights, kv_all,
):
    del in0, in1, in2, in3
    for slot, ref in enumerate((kv3, kv4, kv5)):
        kv_all[HALF + slot] = ref[...]
    stats_steps(
        place_ref, (ranges, starts), (0, SLAB), (HALF, REACH + 1), False,
        qg_all, kv_all, tops, weights, out_ref,
    )


def combine_stats(st_refs, lse_buf, delta_buf):
    stats = [ref[...] for ref in st_refs]
    top = jnp.maximum(
        jnp.maximum(stats[0][0], stats[1][0]), jnp.maximum(stats[2][0], stats[3][0])
    )
    total = jnp.zeros_like(top)
    dot = jnp.zeros_like(top)
    for st in stats:
        factor = jnp.exp2(st[0] - top)
        total = total + st[1] * factor
        dot = dot + st[2] * factor
    lse_buf[...] = top + jnp.log2(total)
    delta_buf[...] = dot / total


def visit_step(j, k, rels, ranges, data, dqt, acc):
    lse_buf, delta_buf, tops, weights, qg_all, kv_all = data
    keys_t = kv_all[k, :, :HD].T

    def per_block(rel, _):
        qb = j ^ rel

        @pl.when((k >= ranges[2 * rel]) & (k <= ranges[2 * rel + 1]))
        def _():
            values = kv_all[k, :, HD:]

            def grad_of(h):
                return qg_all[rel, :, (GROUP + h) * HD : (GROUP + h + 1) * HD]

            dk = dv = None
            ahead = dot_nt(values, grad_of(0))
            for h in range(GROUP):
                dp = ahead
                if h + 1 < GROUP:
                    ahead = dot_nt(values, grad_of(h + 1))
                q = qg_all[rel, :, h * HD : (h + 1) * HD]
                lse = lse_buf[pl.ds(qb * GROUP + h, 1), :]
                delta = delta_buf[pl.ds(qb * GROUP + h, 1), :]
                factor = jnp.exp2(tops[k, pl.ds(rel * GROUP + h, 1), :] - lse)
                p = weights[rel * (REACH + 1) + k, h].astype(F32) * factor
                ds = p * (dp - delta)
                pb = p.astype(BF16)
                dsb = ds.astype(BF16)
                dv_add, dk_add = dot_nn(pb, grad_of(h)), dot_nn(dsb, q)
                dv = dv_add if dv is None else dv + dv_add
                dk = dk_add if dk is None else dk + dk_add
                dqt[rel * GROUP + h] += dot_nn(keys_t, dsb)
            acc[:, :HD] += dk
            acc[:, HD:] += dv

        return 0

    lax.fori_loop(rels[0], rels[1], per_block, 0)


def write_dq(dqt, slot, out_ref):
    for h in range(GROUP):
        dq = (dqt[slot * GROUP + h] * SCALE).astype(BF16)
        out_ref[:, h * HD : (h + 1) * HD] = dq.T


def write_dkv(out_ref, acc):
    out_ref[:, :HD] = (acc[:, :HD] * SCALE).astype(out_ref.dtype)
    out_ref[:, HD:] = acc[:, HD:].astype(out_ref.dtype)


def far_kernel(
    place_ref, ranges, st0, st1, st2, st3, tops, weights, qg_all, kv_all,
    dqt, dkv34, dkv5, acc0_ref, lse_ref, delta_ref, acc,
):
    combine_stats((st0, st1, st2, st3), lse_ref, delta_ref)
    dqt[...] = jnp.zeros_like(dqt)

    def per_step(step, _):
        k = jnp.where(step == 0, 0, REACH + 1 - step)
        acc[...] = jnp.zeros_like(acc)
        visit_step(
            place_ref[1], k, (jnp.where(step == 0, THERE[0], 0), SLAB), ranges,
            (lse_ref, delta_ref, tops, weights, qg_all, kv_all), dqt, acc,
        )

        @pl.when(step == 0)
        def _():
            acc0_ref[...] = acc[...]

        for slot, ref in enumerate((dkv5, dkv34.at[1], dkv34.at[0])):

            @pl.when(step == slot + 1)
            def _():
                write_dkv(ref, acc)

        return 0

    lax.fori_loop(0, HALF + 1, per_step, 0)


def there_kernel(
    place_ref, ranges, dqt_in, lse_ref, delta_ref, tops, weights, qg_all, kv_all,
    dqt, keep_ref, send_ref, acc_ref, acc,
):
    del dqt_in

    def per_step(step, _):
        k = 2 - step
        acc[...] = jnp.zeros_like(acc)
        visit_step(
            place_ref[1], k, THERE, ranges,
            (lse_ref, delta_ref, tops, weights, qg_all, kv_all), dqt, acc,
        )
        acc_ref[k - 1] = acc[...]
        return 0

    lax.fori_loop(0, 2, per_step, 0)
    write_dq(dqt, 2, keep_ref)
    write_dq(dqt, 3, send_ref)


def here_kernel(
    place_ref, ranges, dqt_in, lse_ref, delta_ref, tops, weights, qg_all, kv_all, acc0, acc_near,
    dqt, beside_ref, dkv1, dkv2, acc0_out, acc,
):
    del dqt_in

    def per_step(step, _):
        k = 2 - step

        @pl.when(k > 0)
        def _():
            acc[...] = acc_near[jnp.maximum(k - 1, 0)]

        @pl.when(k == 0)
        def _():
            acc[...] = acc0[...]

        visit_step(
            place_ref[1], k, (jnp.where(k == 0, 1, 0), HERE[1]), ranges,
            (lse_ref, delta_ref, tops, weights, qg_all, kv_all), dqt, acc,
        )

        @pl.when(k == 2)
        def _():
            write_dkv(dkv2, acc)

        @pl.when(k == 1)
        def _():
            write_dkv(dkv1, acc)

        return 0

    lax.fori_loop(0, 3, per_step, 0)
    acc0_out[...] = acc[...]
    write_dq(dqt, 1, beside_ref)


def own_kernel(
    place_ref, ranges, dqt_in, lse_ref, delta_ref, tops, weights, qg_all, kv_all, acc0,
    dqt, dq_ref, dkv_ref, acc,
):
    del dqt_in
    acc[...] = acc0[...]
    visit_step(
        place_ref[1], jnp.int32(0), (0, 1), ranges,
        (lse_ref, delta_ref, tops, weights, qg_all, kv_all), dqt, acc,
    )
    write_dkv(dkv_ref, acc)
    write_dq(dqt, 0, dq_ref)


def pair_kernel(keep, got, out_ref):
    out_ref[...] = (keep[...].astype(F32) + got[...].astype(F32)).astype(BF16)


def merge_kernel(keep, beside, across, dkv0, got1, got2, got5, out_ref):
    parts, part = out_ref.shape[:2]
    width = GROUP * HD
    dkv = dkv0[...] + got1[...].astype(F32) + got2[...].astype(F32)
    dkv = dkv + got5[...].astype(F32)
    dq = keep[...].astype(F32) + beside[...].astype(F32) + across[...].astype(F32)
    out_ref[:, :, :width] = dq.astype(BF16).reshape(parts, part, width)
    out_ref[:, :, width:] = dkv.astype(BF16).reshape(parts, part, 2 * HD)


def finish_kernel(got, q_ref, k_ref, v_ref):
    width = GROUP * HD
    for t in range(got.shape[0]):
        q_ref[:, t * width : (t + 1) * width] = got[t, :, :width]
        k_ref[:, t * HD : (t + 1) * HD] = got[t, :, width : width + HD]
        v_ref[:, t * HD : (t + 1) * HD] = got[t, :, width + HD :]


SMEM_SPEC = pl.BlockSpec(memory_space=pltpu.SMEM)
VMEM_SPEC = pl.BlockSpec(memory_space=pltpu.VMEM)


def call(kernel, name, outs, scratch, *args, scalars=2, aliases=None, smem_outs=0):
    return pl.pallas_call(
        kernel,
        out_shape=tuple(jax.ShapeDtypeStruct(shape, dtype) for shape, dtype in outs),
        in_specs=[SMEM_SPEC] * scalars + [VMEM_SPEC] * (len(args) - scalars),
        out_specs=(SMEM_SPEC,) * smem_outs + (VMEM_SPEC,) * (len(outs) - smem_outs),
        scratch_shapes=[pltpu.VMEM(shape, dtype) for shape, dtype in scratch],
        input_output_aliases=aliases or {},
        compiler_params=pltpu.CompilerParams(vmem_limit_bytes=VMEM_LIMIT),
        cost_estimate=pl.CostEstimate(flops=1, bytes_accessed=1, transcendentals=0),
        name=name,
    )(*args)


QG_ALL = ((SLAB, ROWS, 2 * GROUP * HD), BF16)
KV_ALL = ((REACH + 1, ROWS, 2 * HD), BF16)
STATS = ((3, SLAB * GROUP, ROWS), F32)
TOPS = ((REACH + 1, SLAB * GROUP, ROWS), F32)
WEIGHTS = ((SLAB * (REACH + 1), GROUP, ROWS, ROWS), BF16)
RANGES = ((2 * SLAB,), jnp.int32)
STARTS = ((2 * SLAB, ROWS), jnp.int32)
ROW_STATS = ((SLAB * GROUP, ROWS), F32)
DQT = ((SLAB * GROUP, HD, ROWS), F32)
ACC = ((ROWS, 2 * HD), F32)
DKV = ((ROWS, 2 * HD), BF16)
DQ = ((ROWS, GROUP * HD), BF16)


def flip(x, axis):
    return lax.ppermute(x, axis, [(0, 1), (1, 0)])


def shift(x, by, slabs):
    pairs = [(i, i + by) for i in range(slabs) if 0 <= i + by < slabs]
    return lax.ppermute(x, "z", pairs)


def wrapped(x, by, sources, slabs):
    return lax.ppermute(x, "z", [(i, (i + by) % slabs) for i in sources])


def shift_last(x, by, slabs):
    last = SLAB - 1
    pairs = [
        (i * SLAB + last, (i + by) * SLAB + last) for i in range(slabs) if 0 <= i + by < slabs
    ]
    return lax.ppermute(x, ("z", "y", "core"), pairs)


def local(queries, keys, values, grad_out, doc_lengths):
    z = lax.axis_index("z")
    j = lax.axis_index(("y", "core"))
    slabs = lax.axis_size("z")
    place = jnp.stack((z, j)).astype(jnp.int32)

    qg, kv = pl.pallas_call(
        pack_kernel,
        out_shape=(
            jax.ShapeDtypeStruct((ROWS, 2 * GROUP * HD), BF16),
            jax.ShapeDtypeStruct((ROWS, 2 * HD), BF16),
        ),
        in_specs=[pl.BlockSpec(memory_space=pltpu.HBM)] * 4,
        out_specs=(VMEM_SPEC,) * 2,
        scratch_shapes=[pltpu.SemaphoreType.DMA((4,))],
        compiler_params=pltpu.CompilerParams(vmem_limit_bytes=56 * 1024 * 1024),
        cost_estimate=pl.CostEstimate(flops=1, bytes_accessed=1, transcendentals=0),
        name="pack",
    )(queries, grad_out, keys, values)
    across = flip(qg, "y")
    ahead = [i for i in range(slabs) if i + 4 < slabs]
    kv_by = wrapped(kv, -2, ahead, slabs)
    kv5 = shift_last(kv, 5, slabs)
    kv1 = shift(kv, 1, slabs)
    kv2 = shift(kv, 2, slabs)
    beside = flip(qg, "core")

    ranges, starts, stats, tops, weights, qg_all, kv_all = call(
        first_stats_kernel, "first_statistics",
        [RANGES, STARTS, STATS, TOPS, WEIGHTS, QG_ALL, KV_ALL], [],
        place, doc_lengths, qg, beside, kv, smem_outs=1,
    )
    across, kv_by, kv5, kv1, kv2, stats = lax.optimization_barrier(
        (across, kv_by, kv5, kv1, kv2, stats)
    )
    kv3 = shift(kv2, 1, slabs)
    kv4 = wrapped(kv_by, -2, [(i - 2) % slabs for i in ahead], slabs)
    both = flip(across, "core")
    stats, tops, weights, kv_all = call(
        here_stats_kernel, "here_statistics", [STATS, TOPS, WEIGHTS, KV_ALL], [],
        place, ranges, stats, tops, weights, kv_all, starts, qg_all, kv1, kv2,
        aliases={2: 0, 3: 1, 4: 2, 5: 3},
    )
    stats, tops, weights, qg_all = call(
        there_stats_kernel, "there_statistics", [STATS, TOPS, WEIGHTS, QG_ALL], [],
        place, ranges, stats, tops, weights, qg_all, starts, kv_all, across, both,
        aliases={2: 0, 3: 1, 4: 2, 5: 3},
    )
    stats, tops, weights, kv_all = call(
        far_stats_kernel, "far_statistics", [STATS, TOPS, WEIGHTS, KV_ALL], [],
        place, ranges, stats, tops, weights, kv_all, starts, qg_all, kv3, kv4, kv5,
        aliases={2: 0, 3: 1, 4: 2, 5: 3},
    )
    stats_y = flip(stats, "y")
    stats_c = flip(stats, "core")
    stats_yc = flip(stats_y, "core")

    data = (tops, weights, qg_all, kv_all)
    dqt, dkv34, dkv5, acc0, lse, delta = call(
        far_kernel, "far_gradients",
        [DQT, ((2,) + DKV[0], BF16), DKV, ACC, ROW_STATS, ROW_STATS], [ACC],
        place, ranges, stats, stats_c, stats_y, stats_yc, *data,
    )
    got_far = shift(dkv34, -2, slabs)
    got5 = shift_last(dkv5, -5, slabs)
    dqt, there_keep, there_send, acc_near = call(
        there_kernel, "there_gradients", [DQT, DQ, DQ, ((2,) + ACC[0], F32)], [ACC],
        place, ranges, dqt, lse, delta, *data, aliases={2: 0},
    )
    there_got = flip(there_send, "core")
    dqt, dq_beside, dkv1, dkv2, acc0 = call(
        here_kernel, "here_gradients", [DQT, DQ, ACC, ACC, ACC], [ACC],
        place, ranges, dqt, lse, delta, *data, acc0, acc_near, aliases={2: 0},
    )
    dkv1 = (dkv1 + got_far[0].astype(F32)).astype(BF16)
    dkv2 = (dkv2 + got_far[1].astype(F32)).astype(BF16)
    there_got, dkv1, dkv2 = lax.optimization_barrier((there_got, dkv1, dkv2))
    dq_pair, = call(
        pair_kernel, "pair", [DQ], [], there_keep, there_got, scalars=0
    )
    dq_across = flip(dq_pair, "y")
    dq_beside = flip(dq_beside, "core")
    got1 = shift(dkv1, -1, slabs)
    got2 = shift(dkv2, -2, slabs)
    _, dq_keep, dkv0 = call(
        own_kernel, "own_gradients", [DQT, DQ, ACC], [ACC],
        place, ranges, dqt, lse, delta, *data, acc0, aliases={2: 0},
    )

    tp = lax.axis_size("tp")
    part = ROWS // tp
    width = GROUP * HD
    whole, = call(
        merge_kernel, "merge", [((tp, part, width + 2 * HD), BF16)], [],
        dq_keep, dq_beside, dq_across, dkv0, got1, got2, got5, scalars=0,
    )
    got = lax.all_to_all(whole, "tp", split_axis=0, concat_axis=0, tiled=True)
    return call(
        finish_kernel, "finish",
        [((part, tp * width), BF16), ((part, tp * HD), BF16), ((part, tp * HD), BF16)], [],
        got, scalars=0,
    )


def solution(mesh):
    tp = mesh.shape["tp"]
    inner = Mesh(mesh.devices.reshape(-1, 2, 2, tp), ("z", "y", "core", "tp"))
    tokens = ("z", "y", "core")
    in_specs = (P(tokens, "tp"),) * 4 + (P(),)
    out_specs = (P(tokens + ("tp",), None),) * 3
    return jax.shard_map(local, mesh=inner, in_specs=in_specs, out_specs=out_specs, check_vma=False)
```

```python
import math

import jax
import jax.numpy as jnp
from jax import lax
from jax.experimental import pallas as pl
from jax.experimental.pallas import tpu as pltpu
from jax.sharding import Mesh, PartitionSpec as P

HD = 128
GROUP = 4
ROWS = 256
SLAB = 4
REACH = 5
HALF = 3
HERE = (0, 2)
THERE = (2, 4)
DOC_COUNT = 17
SCALE = HD ** -0.5
SCALE2 = SCALE * math.log2(math.e)
MASKED = -1e30
EMPTY = -1e29
VMEM_LIMIT = 16 * 1024 * 1024
NT = (((1,), (1,)), ((), ()))
NN = (((1,), (0,)), ((), ()))
F32 = jnp.float32
BF16 = jnp.bfloat16


def dot_nt(a, b):
    return lax.dot_general(a, b, NT, preferred_element_type=F32)


def dot_nn(a, b):
    return lax.dot_general(a, b, NN, preferred_element_type=F32)


def start_of(doc_ref, positions):
    end = jnp.int32(0)
    starts = jnp.zeros_like(positions)
    for doc in range(DOC_COUNT):
        length = doc_ref[doc]
        end = end + length
        starts = starts + jnp.where(end <= positions, length, 0)
    return starts


def find_starts(place_ref, doc_ref, starts_ref, ranges_ref):
    z, j = place_ref[0], place_ref[1]
    for rel in range(SLAB):
        qb = j ^ rel
        first = start_of(doc_ref, (SLAB * z + qb) * ROWS) // ROWS
        ranges_ref[2 * rel] = jnp.where(j <= qb, 0, 1)
        ranges_ref[2 * rel + 1] = z - jnp.maximum((first - j + SLAB - 1) >> 2, 0)
        starts_ref[rel : rel + 1, :] = start_of(doc_ref, query_positions(z, qb))


def query_positions(z, qb):
    return (SLAB * z + qb) * ROWS + lax.broadcasted_iota(jnp.int32, (1, ROWS), 1)


def pack_kernel(q_ref, g_ref, k_ref, v_ref, qg_ref, kv_ref, sems):
    wide, thin = GROUP * HD, HD
    copies = [
        pltpu.make_async_copy(k_ref, kv_ref.at[:, :thin], sems.at[0]),
        pltpu.make_async_copy(v_ref, kv_ref.at[:, thin:], sems.at[1]),
        pltpu.make_async_copy(q_ref, qg_ref.at[:, :wide], sems.at[2]),
        pltpu.make_async_copy(g_ref, qg_ref.at[:, wide:], sems.at[3]),
    ]
    for copy in copies:
        copy.start()
    for copy in copies:
        copy.wait()


def stats_steps(place_ref, where, rels, steps, fresh, qg, kv, tops, weights, out_ref):
    z, j = place_ref[0], place_ref[1]
    ranges, starts_ref = where

    def per_block(rel, _):
        qb = j ^ rel
        positions = query_positions(z, qb)
        starts = starts_ref[pl.ds(rel, 1), :]

        def per_step(k, carry):
            key_pos = lax.broadcasted_iota(jnp.int32, (ROWS, ROWS), 0)
            offset = (SLAB * (z - k) + j) * ROWS
            mask = (key_pos >= starts - offset) & (key_pos <= positions - offset)
            keys = kv[k, :, :HD]
            values = kv[k, :, HD:]

            def products(h):
                q = qg[rel, :, h * HD : (h + 1) * HD]
                g = qg[rel, :, (GROUP + h) * HD : (GROUP + h + 1) * HD]
                return dot_nt(keys, q), dot_nt(values, g)

            new = []
            ahead = products(0)
            for h in range(GROUP):
                s, dp = ahead
                if h + 1 < GROUP:
                    ahead = products(h + 1)
                top, total, dot = carry[3 * h : 3 * h + 3]
                s = jnp.where(mask, s * SCALE2, MASKED)
                new_top = jnp.maximum(top, jnp.max(s, axis=0, keepdims=True))
                p = jnp.exp2(s - new_top)
                weights[rel * (REACH + 1) + k, h] = p.astype(BF16)
                tops[k, pl.ds(rel * GROUP + h, 1), :] = new_top
                factor = jnp.exp2(top - new_top)
                new += [
                    new_top,
                    total * factor + jnp.sum(p, axis=0, keepdims=True),
                    dot * factor + jnp.sum(p * dp, axis=0, keepdims=True),
                ]
            return tuple(new)

        if fresh:
            zero = jnp.zeros((1, ROWS), F32)
            init = (jnp.full((1, ROWS), EMPTY, F32), zero, zero) * GROUP
        else:
            init = tuple(
                out_ref[part, pl.ds(qb * GROUP + h, 1), :]
                for h in range(GROUP)
                for part in range(3)
            )
        first = jnp.maximum(ranges[2 * rel], steps[0])
        end = jnp.minimum(ranges[2 * rel + 1] + 1, steps[1])
        done = lax.fori_loop(first, end, per_step, init)
        for h in range(GROUP):
            for part in range(3):
                out_ref[part, pl.ds(qb * GROUP + h, 1), :] = done[3 * h + part]
        return 0

    lax.fori_loop(rels[0], rels[1], per_block, 0)


def first_stats_kernel(
    place_ref, doc_ref, qg0, qg1, kv0, ranges, starts, out_ref, tops, weights, qg_all, kv_all
):
    find_starts(place_ref, doc_ref, starts, ranges)
    qg_all[0] = qg0[...]
    qg_all[1] = qg1[...]
    kv_all[0] = kv0[...]
    stats_steps(
        place_ref, (ranges, starts), HERE, (0, 1), True, qg_all, kv_all, tops, weights, out_ref
    )


def here_stats_kernel(
    place_ref, ranges, in0, in1, in2, in3, starts, qg_all, kv1, kv2, out_ref, tops, weights, kv_all
):
    del in0, in1, in2, in3
    kv_all[1] = kv1[...]
    kv_all[2] = kv2[...]
    stats_steps(
        place_ref, (ranges, starts), HERE, (1, HALF), False,
        qg_all, kv_all, tops, weights, out_ref,
    )


def there_stats_kernel(
    place_ref, ranges, in0, in1, in2, in3, starts, kv_all, qg2, qg3, out_ref, tops, weights, qg_all
):
    del in0, in1, in2, in3
    qg_all[2] = qg2[...]
    qg_all[3] = qg3[...]
    stats_steps(
        place_ref, (ranges, starts), THERE, (0, HALF), True,
        qg_all, kv_all, tops, weights, out_ref,
    )


def far_stats_kernel(
    place_ref, ranges, in0, in1, in2, in3, starts, qg_all, kv3, kv4, kv5,
    out_ref, tops, weights, kv_all,
):
    del in0, in1, in2, in3
    for slot, ref in enumerate((kv3, kv4, kv5)):
        kv_all[HALF + slot] = ref[...]
    stats_steps(
        place_ref, (ranges, starts), (0, SLAB), (HALF, REACH + 1), False,
        qg_all, kv_all, tops, weights, out_ref,
    )


def combine_stats(st_refs, lse_buf, delta_buf):
    stats = [ref[...] for ref in st_refs]
    top = jnp.maximum(
        jnp.maximum(stats[0][0], stats[1][0]), jnp.maximum(stats[2][0], stats[3][0])
    )
    total = jnp.zeros_like(top)
    dot = jnp.zeros_like(top)
    for st in stats:
        factor = jnp.exp2(st[0] - top)
        total = total + st[1] * factor
        dot = dot + st[2] * factor
    lse_buf[...] = top + jnp.log2(total)
    delta_buf[...] = dot / total


def visit_step(j, k, rels, ranges, data, dqt, acc):
    lse_buf, delta_buf, tops, weights, qg_all, kv_all = data
    keys_t = kv_all[k, :, :HD].T

    def per_block(rel, _):
        qb = j ^ rel

        @pl.when((k >= ranges[2 * rel]) & (k <= ranges[2 * rel + 1]))
        def _():
            values = kv_all[k, :, HD:]

            def grad_of(h):
                return qg_all[rel, :, (GROUP + h) * HD : (GROUP + h + 1) * HD]

            dk = dv = None
            ahead = dot_nt(values, grad_of(0))
            for h in range(GROUP):
                dp = ahead
                if h + 1 < GROUP:
                    ahead = dot_nt(values, grad_of(h + 1))
                q = qg_all[rel, :, h * HD : (h + 1) * HD]
                lse = lse_buf[pl.ds(qb * GROUP + h, 1), :]
                delta = delta_buf[pl.ds(qb * GROUP + h, 1), :]
                factor = jnp.exp2(tops[k, pl.ds(rel * GROUP + h, 1), :] - lse)
                p = weights[rel * (REACH + 1) + k, h].astype(F32) * factor
                ds = p * (dp - delta)
                pb = p.astype(BF16)
                dsb = ds.astype(BF16)
                dv_add, dk_add = dot_nn(pb, grad_of(h)), dot_nn(dsb, q)
                dv = dv_add if dv is None else dv + dv_add
                dk = dk_add if dk is None else dk + dk_add
                dqt[rel * GROUP + h] += dot_nn(keys_t, dsb)
            acc[:, :HD] += dk
            acc[:, HD:] += dv

        return 0

    lax.fori_loop(rels[0], rels[1], per_block, 0)


def write_dq(dqt, slot, out_ref):
    for h in range(GROUP):
        dq = (dqt[slot * GROUP + h] * SCALE).astype(BF16)
        out_ref[:, h * HD : (h + 1) * HD] = dq.T


def write_dkv(out_ref, acc):
    out_ref[:, :HD] = (acc[:, :HD] * SCALE).astype(out_ref.dtype)
    out_ref[:, HD:] = acc[:, HD:].astype(out_ref.dtype)


def far_kernel(
    place_ref, ranges, st0, st1, st2, st3, tops, weights, qg_all, kv_all,
    dqt, dkv34, dkv5, lse_ref, delta_ref, acc,
):
    combine_stats((st0, st1, st2, st3), lse_ref, delta_ref)
    dqt[...] = jnp.zeros_like(dqt)

    def per_step(step, _):
        k = REACH - step
        acc[...] = jnp.zeros_like(acc)
        visit_step(
            place_ref[1], k, (0, SLAB), ranges,
            (lse_ref, delta_ref, tops, weights, qg_all, kv_all), dqt, acc,
        )

        for slot, ref in enumerate((dkv5, dkv34.at[1], dkv34.at[0])):

            @pl.when(step == slot)
            def _():
                write_dkv(ref, acc)

        return 0

    lax.fori_loop(0, HALF, per_step, 0)


def there_kernel(
    place_ref, ranges, dqt_in, lse_ref, delta_ref, tops, weights, qg_all, kv_all,
    dqt, keep_ref, send_ref, acc_ref, acc,
):
    del dqt_in

    def per_step(step, _):
        k = 2 - step
        acc[...] = jnp.zeros_like(acc)
        visit_step(
            place_ref[1], k, THERE, ranges,
            (lse_ref, delta_ref, tops, weights, qg_all, kv_all), dqt, acc,
        )
        acc_ref[k] = acc[...]
        return 0

    lax.fori_loop(0, HALF, per_step, 0)
    write_dq(dqt, 2, keep_ref)
    write_dq(dqt, 3, send_ref)


def here_kernel(
    place_ref, ranges, dqt_in, lse_ref, delta_ref, tops, weights, qg_all, kv_all, acc_near,
    dqt, beside_ref, dkv1, dkv2, acc0_out, acc,
):
    del dqt_in

    def per_step(step, _):
        k = 2 - step
        acc[...] = acc_near[k]
        visit_step(
            place_ref[1], k, (jnp.where(k == 0, 1, 0), HERE[1]), ranges,
            (lse_ref, delta_ref, tops, weights, qg_all, kv_all), dqt, acc,
        )

        @pl.when(k == 2)
        def _():
            write_dkv(dkv2, acc)

        @pl.when(k == 1)
        def _():
            write_dkv(dkv1, acc)

        return 0

    lax.fori_loop(0, HALF, per_step, 0)
    acc0_out[...] = acc[...]
    write_dq(dqt, 1, beside_ref)


def own_kernel(
    place_ref, ranges, dqt_in, lse_ref, delta_ref, tops, weights, qg_all, kv_all, acc0,
    dqt, dq_ref, dkv_ref, acc,
):
    del dqt_in
    acc[...] = acc0[...]
    visit_step(
        place_ref[1], jnp.int32(0), (0, 1), ranges,
        (lse_ref, delta_ref, tops, weights, qg_all, kv_all), dqt, acc,
    )
    write_dkv(dkv_ref, acc)
    write_dq(dqt, 0, dq_ref)


def pair_kernel(keep, got, out_ref):
    out_ref[...] = (keep[...].astype(F32) + got[...].astype(F32)).astype(BF16)


def merge_kernel(keep, beside, across, dkv0, got1, got2, got5, out_ref):
    parts, part = out_ref.shape[:2]
    width = GROUP * HD
    dkv = dkv0[...] + got1[...].astype(F32) + got2[...].astype(F32)
    dkv = dkv + got5[...].astype(F32)
    dq = keep[...].astype(F32) + beside[...].astype(F32) + across[...].astype(F32)
    out_ref[:, :, :width] = dq.astype(BF16).reshape(parts, part, width)
    out_ref[:, :, width:] = dkv.astype(BF16).reshape(parts, part, 2 * HD)


def finish_kernel(got, q_ref, k_ref, v_ref):
    width = GROUP * HD
    for t in range(got.shape[0]):
        q_ref[:, t * width : (t + 1) * width] = got[t, :, :width]
        k_ref[:, t * HD : (t + 1) * HD] = got[t, :, width : width + HD]
        v_ref[:, t * HD : (t + 1) * HD] = got[t, :, width + HD :]


SMEM_SPEC = pl.BlockSpec(memory_space=pltpu.SMEM)
VMEM_SPEC = pl.BlockSpec(memory_space=pltpu.VMEM)


def call(kernel, name, outs, scratch, *args, scalars=2, aliases=None, smem_outs=0):
    return pl.pallas_call(
        kernel,
        out_shape=tuple(jax.ShapeDtypeStruct(shape, dtype) for shape, dtype in outs),
        in_specs=[SMEM_SPEC] * scalars + [VMEM_SPEC] * (len(args) - scalars),
        out_specs=(SMEM_SPEC,) * smem_outs + (VMEM_SPEC,) * (len(outs) - smem_outs),
        scratch_shapes=[pltpu.VMEM(shape, dtype) for shape, dtype in scratch],
        input_output_aliases=aliases or {},
        compiler_params=pltpu.CompilerParams(vmem_limit_bytes=VMEM_LIMIT),
        cost_estimate=pl.CostEstimate(flops=1, bytes_accessed=1, transcendentals=0),
        name=name,
    )(*args)


QG_ALL = ((SLAB, ROWS, 2 * GROUP * HD), BF16)
KV_ALL = ((REACH + 1, ROWS, 2 * HD), BF16)
STATS = ((3, SLAB * GROUP, ROWS), F32)
TOPS = ((REACH + 1, SLAB * GROUP, ROWS), F32)
WEIGHTS = ((SLAB * (REACH + 1), GROUP, ROWS, ROWS), BF16)
RANGES = ((2 * SLAB,), jnp.int32)
STARTS = ((2 * SLAB, ROWS), jnp.int32)
ROW_STATS = ((SLAB * GROUP, ROWS), F32)
DQT = ((SLAB * GROUP, HD, ROWS), F32)
ACC = ((ROWS, 2 * HD), F32)
DKV = ((ROWS, 2 * HD), BF16)
DQ = ((ROWS, GROUP * HD), BF16)


def flip(x, axis):
    return lax.ppermute(x, axis, [(0, 1), (1, 0)])


def shift(x, by, slabs):
    pairs = [(i, i + by) for i in range(slabs) if 0 <= i + by < slabs]
    return lax.ppermute(x, "z", pairs)


def wrapped(x, by, sources, slabs):
    return lax.ppermute(x, "z", [(i, (i + by) % slabs) for i in sources])


def shift_last(x, by, slabs):
    last = SLAB - 1
    pairs = [
        (i * SLAB + last, (i + by) * SLAB + last) for i in range(slabs) if 0 <= i + by < slabs
    ]
    return lax.ppermute(x, ("z", "y", "core"), pairs)


def local(queries, keys, values, grad_out, doc_lengths):
    z = lax.axis_index("z")
    j = lax.axis_index(("y", "core"))
    slabs = lax.axis_size("z")
    place = jnp.stack((z, j)).astype(jnp.int32)

    qg, kv = pl.pallas_call(
        pack_kernel,
        out_shape=(
            jax.ShapeDtypeStruct((ROWS, 2 * GROUP * HD), BF16),
            jax.ShapeDtypeStruct((ROWS, 2 * HD), BF16),
        ),
        in_specs=[pl.BlockSpec(memory_space=pltpu.HBM)] * 4,
        out_specs=(VMEM_SPEC,) * 2,
        scratch_shapes=[pltpu.SemaphoreType.DMA((4,))],
        compiler_params=pltpu.CompilerParams(vmem_limit_bytes=56 * 1024 * 1024),
        cost_estimate=pl.CostEstimate(flops=1, bytes_accessed=1, transcendentals=0),
        name="pack",
    )(queries, grad_out, keys, values)
    across = flip(qg, "y")
    ahead = [i for i in range(slabs) if i + 4 < slabs]
    kv_by = wrapped(kv, -2, ahead, slabs)
    kv5 = shift_last(kv, 5, slabs)
    kv1 = shift(kv, 1, slabs)
    kv2 = shift(kv, 2, slabs)
    beside = flip(qg, "core")

    ranges, starts, stats, tops, weights, qg_all, kv_all = call(
        first_stats_kernel, "first_statistics",
        [RANGES, STARTS, STATS, TOPS, WEIGHTS, QG_ALL, KV_ALL], [],
        place, doc_lengths, qg, beside, kv, smem_outs=1,
    )
    across, kv_by, kv5, kv1, kv2, stats = lax.optimization_barrier(
        (across, kv_by, kv5, kv1, kv2, stats)
    )
    kv3 = shift(kv2, 1, slabs)
    kv4 = wrapped(kv_by, -2, [(i - 2) % slabs for i in ahead], slabs)
    both = flip(across, "core")
    stats, tops, weights, kv_all = call(
        here_stats_kernel, "here_statistics", [STATS, TOPS, WEIGHTS, KV_ALL], [],
        place, ranges, stats, tops, weights, kv_all, starts, qg_all, kv1, kv2,
        aliases={2: 0, 3: 1, 4: 2, 5: 3},
    )
    stats, tops, weights, qg_all = call(
        there_stats_kernel, "there_statistics", [STATS, TOPS, WEIGHTS, QG_ALL], [],
        place, ranges, stats, tops, weights, qg_all, starts, kv_all, across, both,
        aliases={2: 0, 3: 1, 4: 2, 5: 3},
    )
    stats, tops, weights, kv_all = call(
        far_stats_kernel, "far_statistics", [STATS, TOPS, WEIGHTS, KV_ALL], [],
        place, ranges, stats, tops, weights, kv_all, starts, qg_all, kv3, kv4, kv5,
        aliases={2: 0, 3: 1, 4: 2, 5: 3},
    )
    stats_y = flip(stats, "y")
    stats_c = flip(stats, "core")
    stats_yc = flip(stats_y, "core")

    data = (tops, weights, qg_all, kv_all)
    dqt, dkv34, dkv5, lse, delta = call(
        far_kernel, "far_gradients",
        [DQT, ((2,) + DKV[0], BF16), DKV, ROW_STATS, ROW_STATS], [ACC],
        place, ranges, stats, stats_c, stats_y, stats_yc, *data,
    )
    got_far = shift(dkv34, -2, slabs)
    got5 = shift_last(dkv5, -5, slabs)
    dqt, there_keep, there_send, acc_near = call(
        there_kernel, "there_gradients", [DQT, DQ, DQ, ((HALF,) + ACC[0], F32)], [ACC],
        place, ranges, dqt, lse, delta, *data, aliases={2: 0},
    )
    there_got = flip(there_send, "core")
    dqt, dq_beside, dkv1, dkv2, acc0 = call(
        here_kernel, "here_gradients", [DQT, DQ, ACC, ACC, ACC], [ACC],
        place, ranges, dqt, lse, delta, *data, acc_near, aliases={2: 0},
    )
    dkv1 = (dkv1 + got_far[0].astype(F32)).astype(BF16)
    dkv2 = (dkv2 + got_far[1].astype(F32)).astype(BF16)
    there_got, dkv1, dkv2 = lax.optimization_barrier((there_got, dkv1, dkv2))
    dq_pair, = call(
        pair_kernel, "pair", [DQ], [], there_keep, there_got, scalars=0
    )
    dq_across = flip(dq_pair, "y")
    dq_beside = flip(dq_beside, "core")
    got2 = shift(dkv2, -2, slabs)
    got1 = shift(dkv1, -1, slabs)
    _, dq_keep, dkv0 = call(
        own_kernel, "own_gradients", [DQT, DQ, ACC], [ACC],
        place, ranges, dqt, lse, delta, *data, acc0, aliases={2: 0},
    )

    tp = lax.axis_size("tp")
    part = ROWS // tp
    width = GROUP * HD
    whole, = call(
        merge_kernel, "merge", [((tp, part, width + 2 * HD), BF16)], [],
        dq_keep, dq_beside, dq_across, dkv0, got1, got2, got5, scalars=0,
    )
    got = lax.all_to_all(whole, "tp", split_axis=0, concat_axis=0, tiled=True)
    return call(
        finish_kernel, "finish",
        [((part, tp * width), BF16), ((part, tp * HD), BF16), ((part, tp * HD), BF16)], [],
        got, scalars=0,
    )


def solution(mesh):
    tp = mesh.shape["tp"]
    inner = Mesh(mesh.devices.reshape(-1, 2, 2, tp), ("z", "y", "core", "tp"))
    tokens = ("z", "y", "core")
    in_specs = (P(tokens, "tp"),) * 4 + (P(),)
    out_specs = (P(tokens + ("tp",), None),) * 3
    return jax.shard_map(local, mesh=inner, in_specs=in_specs, out_specs=out_specs, check_vma=False)
```
